256 devices in a mesh: row: 16 (over y_lo, x, core), col: 16 (over z, y_hi).
Axes of the slice: x: 4, y: 4 (y_hi: 2, y_lo: 2; y = y_hi * 2 + y_lo), z: 8, core: 2. Of those that a mesh axis runs over, the one named last changes fastest.
Arguments:
- pair_act: float32 [768, 768, 128], P('row', 'col'), may hold values from -6 to 6
- residue_mask: int32 [768], replicated, may hold values 0 or 1
- norm_in_gain: float32 [128], replicated, may hold values from 0.1 to 1.9
- norm_in_bias: float32 [128], replicated, may hold values from -3 to 3
- proj_in: bfloat16 [128, 640], replicated, may hold values from -0.5 to 0.5
- proj_bias: float32 [640], replicated, may hold values from -3 to 3
- norm_out_gain: float32 [128], replicated, may hold values from 0.1 to 1.9
- norm_out_bias: float32 [128], replicated, may hold values from -3 to 3
- proj_out: bfloat16 [128, 128], replicated, may hold values from -0.5 to 0.5
- out_bias: float32 [128], replicated, may hold values from -3 to 3
Outputs:
- update: float32 [768, 768, 128], P('row', 'col')
The draws below stay inside these ranges and needn't reach their ends.
All inputs are finite; a program needn't handle non-finite values.
Results may differ from the reference program's by a relative error of at most 0.0028.
Values may be sent and summed in bfloat16 or wider, within the bound.
No kernel may reach another device: no remote copies, remote signals or barrier semaphores. Data moves between devices by JAX's collectives and lax.ppermute only.
A program may use at most 128 MiB of HBM per device.

```python
import jax
import jax.numpy as jnp
from jax import lax

C = 128
CH = 128
N = 768


def plant(drawn, stream_key, low, high):
    longest = drawn.shape.index(max(drawn.shape))
    spots = []
    for shift in (0, 1):
        where = [jax.random.randint(jax.random.fold_in(stream_key, axis), (), 0, length) for axis, length in enumerate(drawn.shape)]
        where[longest] = (where[longest] + shift) % drawn.shape[longest]
        spots.append(tuple(where))
    return drawn.at[spots[0]].set(low).at[spots[1]].set(high)


def steps_of(own_key, dims, split, least, top_value):
    level = 1.0
    for position, parts in split:
        draws = jax.random.uniform(jax.random.fold_in(jax.random.fold_in(own_key, 6), position), (parts,), jnp.float32, least / len(split), top_value / len(split))
        level = level * jnp.repeat(jnp.exp(draws), dims[position] // parts).reshape((-1,) + (1,) * (len(dims) - 1 - position))
    return level


def normal_values(rng, dims, deviation, most, shards=(), kind=jnp.bfloat16):
    result = deviation * jax.random.normal(rng, dims, jnp.float32)
    if shards:
        result = result * steps_of(rng, dims, shards, -0.22, 0.18)
    return jnp.clip(result, -most, most).astype(kind)


def setup_inputs(seed: int = 0) -> dict:
    streams_of = jax.random.split(jax.random.key(seed), 11)
    pair_act = normal_values(streams_of[0], (N, N, C), 1.0, 6.0, ((0, 16), (1, 16)), jnp.float32)
    residue_mask = plant((jax.random.randint(streams_of[1], (N,), 0, 8) < 7).astype(jnp.int32), jax.random.fold_in(streams_of[1], 1), 0, 1)
    norm_in_gain = jnp.clip(1.0 + 0.18 * jax.random.normal(streams_of[2], (C,), jnp.float32), 0.1, 1.9)
    norm_in_bias = normal_values(streams_of[3], (C,), 0.5, 3.0, (), jnp.float32)
    proj_in = normal_values(streams_of[4], (C, 4 * CH + C), C ** -0.5, 0.5)
    proj_bias = normal_values(streams_of[5], (4 * CH + C,), 0.5, 3.0, (), jnp.float32)
    norm_out_gain = jnp.clip(1.0 + 0.18 * jax.random.normal(streams_of[6], (CH,), jnp.float32), 0.1, 1.9)
    norm_out_bias = normal_values(streams_of[7], (CH,), 0.5, 3.0, (), jnp.float32)
    proj_out = normal_values(streams_of[8], (CH, C), CH ** -0.5, 0.5)
    out_bias = normal_values(streams_of[9], (C,), 0.5, 3.0, (), jnp.float32)
    return dict(pair_act=pair_act, residue_mask=residue_mask, norm_in_gain=norm_in_gain, norm_in_bias=norm_in_bias, proj_in=proj_in, proj_bias=proj_bias, norm_out_gain=norm_out_gain, norm_out_bias=norm_out_bias, proj_out=proj_out, out_bias=out_bias)


def layer_norm(values, gain_vec, bias_vec):
    center = lax.optimization_barrier(jnp.mean(values, axis=-1, keepdims=True))
    spread = lax.optimization_barrier(jnp.mean(jnp.square(values - center), axis=-1, keepdims=True))
    return (values - center) * lax.rsqrt(spread + 1e-05) * gain_vec + bias_vec

def reference(pair_act, residue_mask, norm_in_gain, norm_in_bias, proj_in, proj_bias, norm_out_gain, norm_out_bias, proj_out, out_bias):
    normed = layer_norm(pair_act, norm_in_gain, norm_in_bias).astype(jnp.bfloat16)
    projected = jnp.dot(normed.reshape(N * N, C), proj_in, preferred_element_type=jnp.float32).reshape(N, N, 4 * CH + C) + proj_bias
    mask_float = residue_mask.astype(jnp.float32)
    pair_mask = (mask_float[:, None] * mask_float[None, :])[:, :, None]
    left_side = (pair_mask * jax.nn.sigmoid(projected[:, :, :CH]) * projected[:, :, CH:2 * CH]).astype(jnp.bfloat16)
    right_side = (pair_mask * jax.nn.sigmoid(projected[:, :, 2 * CH:3 * CH]) * projected[:, :, 3 * CH:4 * CH]).astype(jnp.bfloat16)
    out_gate = jax.nn.sigmoid(projected[:, :, 4 * CH:])
    triangle = jnp.einsum('kic,kjc->ijc', left_side.astype(jnp.float32), right_side.astype(jnp.float32))
    mixed = layer_norm(triangle, norm_out_gain, norm_out_bias).astype(jnp.bfloat16)
    output_lin = jnp.dot(mixed.reshape(N * N, CH), proj_out, preferred_element_type=jnp.float32).reshape(N, N, C) + out_bias
    return out_gate * output_lin
```

```python
import jax
import jax.numpy as jnp
from jax import lax
from jax.sharding import Mesh
from jax.sharding import PartitionSpec as P

CH = 128
ROW = ("y_lo", "x", "core")
COL = ("z", "y_hi")
CHIPS = ("y_lo", "x", "z", "y_hi")
SWAP = [(0, 1), (1, 0)]


def layer_norm(values, gain_vec, bias_vec, axis):
    center = jnp.mean(values, axis=axis, keepdims=True)
    spread = jnp.mean(jnp.square(values - center), axis=axis, keepdims=True)
    return (values - center) * lax.rsqrt(spread + 1e-05) * gain_vec + bias_vec


def body(
    pair_act,
    residue_mask,
    norm_in_gain,
    norm_in_bias,
    proj_in,
    proj_bias,
    norm_out_gain,
    norm_out_bias,
    proj_out,
    out_bias,
):
    rows, cols, chans = pair_act.shape
    block = rows * cols
    n_pair, n_col = lax.axis_size(("y_lo", "x")), lax.axis_size(COL)
    core = lax.axis_index("core")
    flat = pair_act.reshape(block, chans)
    normed = layer_norm(flat, norm_in_gain, norm_in_bias, -1).astype(jnp.bfloat16)
    sides = lax.dot_general(
        proj_in[:, : 4 * CH], normed, (((0,), (1,)), ((), ())), preferred_element_type=jnp.float32
    ) + proj_bias[: 4 * CH, None]
    mask_float = residue_mask.astype(jnp.float32)
    row_mask = lax.dynamic_slice_in_dim(mask_float, lax.axis_index(ROW) * rows, rows)
    col_mask = lax.dynamic_slice_in_dim(mask_float, lax.axis_index(COL) * cols, cols)
    pair_mask = (row_mask[:, None] * col_mask[None, :]).reshape(1, block)
    left = (pair_mask * jax.nn.sigmoid(sides[:CH]) * sides[CH : 2 * CH]).astype(jnp.bfloat16)
    right = (
        pair_mask * jax.nn.sigmoid(sides[2 * CH : 3 * CH]) * sides[3 * CH :]
    ).astype(jnp.bfloat16)
    packed = jnp.stack([left, right], axis=1)
    packed = lax.all_to_all(packed, CHIPS, 0, 0, tiled=True)
    packed = packed.reshape(n_pair, n_col // 2, 2, 2, rows, cols)
    left_m = packed[:, :, :, 0].transpose(0, 3, 2, 1, 4).reshape(n_pair * rows, 2, n_col // 2 * cols)
    right_m = packed[:, :, :, 1].transpose(0, 3, 1, 2, 4).reshape(n_pair * rows, n_col * cols)
    left_mine = lax.dynamic_index_in_dim(left_m, core, 1, keepdims=False)
    left_send = lax.dynamic_index_in_dim(left_m, 1 - core, 1, keepdims=False)
    left_got = lax.ppermute(left_send, "core", SWAP)
    right_got = lax.ppermute(right_m, "core", SWAP)
    dims = (((0,), (0,)), ((), ()))
    triangle = lax.dot_general(left_mine, right_m, dims, preferred_element_type=jnp.float32)
    triangle += lax.dot_general(left_got, right_got, dims, preferred_element_type=jnp.float32)
    triangle = triangle.astype(jnp.bfloat16)
    triangle = triangle.reshape(n_pair, rows, n_col, cols).transpose(0, 2, 1, 3)
    triangle = lax.all_to_all(triangle.reshape(-1, 18, 128), CHIPS, 0, 0, tiled=True)
    triangle = triangle.reshape(CH, block).astype(jnp.float32)
    mixed = layer_norm(triangle, norm_out_gain[:, None], norm_out_bias[:, None], 0)
    high = mixed.astype(jnp.bfloat16)
    low = (mixed - high.astype(jnp.float32)).astype(jnp.bfloat16)
    output_lin = (
        lax.dot_general(high, proj_out, dims, preferred_element_type=jnp.float32)
        + lax.dot_general(low, proj_out, dims, preferred_element_type=jnp.float32)
        + out_bias
    )
    out_gate = jax.nn.sigmoid(
        jnp.dot(normed, proj_in[:, 4 * CH :], preferred_element_type=jnp.float32)
        + proj_bias[4 * CH :]
    )
    return (out_gate * output_lin).reshape(rows, cols, chans)


def solution(mesh):
    fine = Mesh(mesh.devices.reshape(2, 4, 2, 8, 2), ROW + COL)
    return jax.shard_map(
        body,
        mesh=fine,
        in_specs=(P(ROW, COL, None), P(), P(), P(), P(), P(), P(), P(), P(), P()),
        out_specs=P(ROW, COL, None),
        check_vma=False,
    )
```

```python
import jax
import jax.numpy as jnp
from jax import lax
from jax.experimental import pallas as pl
from jax.experimental.pallas import tpu as pltpu
from jax.sharding import Mesh
from jax.sharding import PartitionSpec as P

CH = 128
ROW = ("y_lo", "x", "core")
COL = ("z", "y_hi")
CHIPS = ("y_hi", "z", "y_lo", "x")
SWAP = [(0, 1), (1, 0)]
LANES = 128
SIDE = 48
WIDE = 32
THIN = 16
BLOCK = SIDE * SIDE
THIN_AT = SIDE * WIDE
STEP = 8
F32 = jnp.float32
BF16 = jnp.bfloat16
EPS = 1e-05


def regroup(parts, width):
    lane = lax.broadcasted_iota(jnp.int32, parts[0].shape, 1)
    count = LANES // width
    parts = list(parts)
    hop = count // 2
    while hop:
        shift = hop * width
        low = (lane // shift) % 2 == 0
        nxt = list(parts)
        for g in range(count):
            if g & hop == 0:
                a, b = parts[g], parts[g | hop]
                nxt[g] = jnp.where(low, a, pltpu.roll(b, shift, 1))
                nxt[g | hop] = jnp.where(low, pltpu.roll(a, LANES - shift, 1), b)
        parts = nxt
        hop //= 2
    return parts


def rows_of(act_ref, at):
    block = act_ref[at : at + STEP]
    return jnp.concatenate(
        [
            block[:, :WIDE].reshape(STEP * WIDE, LANES),
            block[:, WIDE:].reshape(STEP * THIN, LANES),
        ],
        axis=0,
    )


def norm_rows(values, gain, bias):
    center = jnp.mean(values, axis=-1, keepdims=True)
    off = values - center
    spread = jnp.mean(jnp.square(off), axis=-1, keepdims=True)
    return (off * lax.rsqrt(spread + EPS) * gain + bias).astype(BF16)


def sides_kernel(act_ref, row_ref, col_ref, gain_ref, bias_ref, w_ref, wb_ref, out_ref, wt_ref):
    wt_ref[...] = w_ref[:, : 4 * CH].T
    lanes = STEP * SIDE
    place = lax.broadcasted_iota(jnp.int32, (SIDE, lanes), 1)
    index = lax.broadcasted_iota(jnp.int32, (SIDE, lanes), 0)
    wide = place < STEP * WIDE
    k_of = jnp.where(wide, place // WIDE, (place - STEP * WIDE) // THIN)
    i_of = jnp.where(wide, place % WIDE, WIDE + (place - STEP * WIDE) % THIN)
    col_mask = jnp.dot(col_ref[...], (i_of == index).astype(F32), preferred_element_type=F32)
    for at in range(0, SIDE, STEP):
        row_mask = jnp.dot(
            row_ref[...], (k_of + at == index).astype(F32), preferred_element_type=F32
        )
        mask = (row_mask * col_mask)[:1]
        normed = norm_rows(rows_of(act_ref, at), gain_ref[...], bias_ref[...])
        for side in range(2):
            both = (
                lax.dot_general(
                    wt_ref[side * 2 * CH : (side + 1) * 2 * CH],
                    normed,
                    (((1,), (1,)), ((), ())),
                    preferred_element_type=F32,
                )
                + wb_ref[side * 2 * CH : (side + 1) * 2 * CH]
            )
            value = (mask * jax.nn.sigmoid(both[:CH]) * both[CH:]).astype(BF16)
            out_ref[side, :, at * WIDE : (at + STEP) * WIDE] = value[:, : STEP * WIDE]
            out_ref[side, :, THIN_AT + at * THIN : THIN_AT + (at + STEP) * THIN] = value[
                :, STEP * WIDE :
            ]


def gate_kernel(act_ref, gain_ref, bias_ref, w_ref, wb_ref, out_ref):
    for at in range(0, SIDE, STEP):
        normed = norm_rows(rows_of(act_ref, at), gain_ref[...], bias_ref[...])
        lin = jnp.dot(normed, w_ref[...], preferred_element_type=F32) + wb_ref[...]
        out_ref[at * SIDE : (at + STEP) * SIDE] = jax.nn.sigmoid(lin)


def gather_k(mine, got, blocks, dst_ref):
    for width, lanes_at, col_at in ((WIDE, 0, 0), (THIN, THIN_AT, blocks * WIDE)):
        count = LANES // width
        for group in range(blocks // count):
            for piece in range(SIDE // count):
                lanes = slice(lanes_at + piece * LANES, lanes_at + (piece + 1) * LANES)
                halves = []
                for ref in (mine, got):
                    parts = []
                    for pair in range(count // 2):
                        row = (group * count + 2 * pair) * 8
                        two = ref[row : row + 16, lanes].astype(F32)
                        parts += [two[:8], two[8:]]
                    halves.append(regroup(parts, width))
                for b in range(count):
                    k = piece * count + b
                    both = jnp.concatenate([halves[0][b], halves[1][b]], axis=0).astype(BF16)
                    dst_ref[
                        16 * k : 16 * (k + 1), col_at + group * LANES : col_at + (group + 1) * LANES
                    ] = both


def triangle_kernel(lm_ref, lg_ref, rm_ref, rg_ref, out_ref, left_ref, right_ref, tri_ref):
    gather_k(lm_ref, lg_ref, 8, left_ref)
    gather_k(rm_ref, rg_ref, 16, right_ref)
    product = lax.dot_general(
        left_ref[...], right_ref[...], (((0,), (0,)), ((), ())), preferred_element_type=F32
    )
    for strip in range(tri_ref.shape[0]):
        tri_ref[strip] = product[:, strip * LANES : (strip + 1) * LANES]
    for width, lanes_at, col_at in ((WIDE, 0, 0), (THIN, THIN_AT, 16 * WIDE)):
        count = LANES // width
        for group in range(16 // count):
            strip = tri_ref.at[col_at // LANES + group]
            for piece in range(SIDE // count):
                parts = []
                for b in range(count):
                    i = piece * count + b
                    if i < WIDE:
                        parts.append(strip[pl.ds(i, 8, stride=WIDE), :])
                    else:
                        parts.append(strip[pl.ds(8 * WIDE + i - WIDE, 8, stride=THIN), :])
                parts = regroup(parts, width)
                for pair in range(count // 2):
                    row = (group * count + 2 * pair) * 8
                    out_ref[
                        row : row + 16, lanes_at + piece * LANES : lanes_at + (piece + 1) * LANES
                    ] = jnp.concatenate(parts[2 * pair : 2 * pair + 2], axis=0).astype(BF16)


def finish_kernel(tri_ref, gate_ref, gain_ref, bias_ref, w_ref, wb_ref, out_ref):
    twice = jnp.concatenate([w_ref[...], w_ref[...]], axis=0)
    for at in range(0, SIDE, STEP):
        tri = jnp.concatenate(
            [
                tri_ref[:, at * WIDE : (at + STEP) * WIDE],
                tri_ref[:, THIN_AT + at * THIN : THIN_AT + (at + STEP) * THIN],
            ],
            axis=1,
        ).astype(F32)
        off = tri - jnp.mean(tri, axis=0, keepdims=True)
        spread = jnp.mean(jnp.square(off), axis=0, keepdims=True)
        mixed = off * lax.rsqrt(spread + EPS) * gain_ref[...] + bias_ref[...]
        high = mixed.astype(BF16)
        low = (mixed - high.astype(F32)).astype(BF16)
        lin = lax.dot_general(
            jnp.concatenate([high, low], axis=0),
            twice,
            (((0,), (0,)), ((), ())),
            preferred_element_type=F32,
        )
        update = gate_ref[at * SIDE : (at + STEP) * SIDE] * (lin + wb_ref[...])
        out_ref[at : at + STEP, :WIDE] = update[: STEP * WIDE].reshape(STEP, WIDE, LANES)
        out_ref[at : at + STEP, WIDE:] = update[STEP * WIDE :].reshape(STEP, THIN, LANES)


def call(kernel, shape, dtype, scratch=(), flops=10**8):
    return pl.pallas_call(
        kernel,
        out_shape=jax.ShapeDtypeStruct(shape, dtype),
        scratch_shapes=scratch,
        compiler_params=pltpu.CompilerParams(vmem_limit_bytes=40 * 2**20),
        cost_estimate=pl.CostEstimate(flops=flops, bytes_accessed=3 * 10**6, transcendentals=0),
    )


def body(
    pair_act,
    residue_mask,
    norm_in_gain,
    norm_in_bias,
    proj_in,
    proj_bias,
    norm_out_gain,
    norm_out_bias,
    proj_out,
    out_bias,
):
    core = lax.axis_index("core")
    mask_float = residue_mask.astype(F32)
    row_mask = lax.dynamic_slice_in_dim(mask_float, lax.axis_index(ROW) * SIDE, SIDE)
    col_mask = lax.dynamic_slice_in_dim(mask_float, lax.axis_index(COL) * SIDE, SIDE)
    gain_in, bias_in = norm_in_gain[None], norm_in_bias[None]
    sides = call(
        sides_kernel, (2, CH, BLOCK), BF16, [pltpu.VMEM((4 * CH, LANES), BF16)]
    )(
        pair_act,
        jnp.broadcast_to(row_mask[None], (8, SIDE)),
        jnp.broadcast_to(col_mask[None], (8, SIDE)),
        gain_in,
        bias_in,
        proj_in,
        proj_bias[:, None],
    )
    packed = sides.transpose(1, 0, 2)
    packed = lax.all_to_all(packed, CHIPS, 0, 0, tiled=True)
    left, right = packed[:, 0], packed[:, 1]
    half = CH // 2
    left_mine = lax.dynamic_slice_in_dim(left, core * half, half)
    left_send = lax.dynamic_slice_in_dim(left, (1 - core) * half, half)
    left_got = lax.ppermute(left_send, "core", SWAP)
    right_got = lax.ppermute(right, "core", SWAP)
    triangle = call(
        triangle_kernel,
        (CH, BLOCK),
        BF16,
        [
            pltpu.VMEM((16 * SIDE, 8 * SIDE), BF16),
            pltpu.VMEM((16 * SIDE, 16 * SIDE), BF16),
            pltpu.VMEM((6, 8 * SIDE, LANES), F32),
        ],
    )(left_mine, left_got, right, right_got)
    gate = call(gate_kernel, (BLOCK, CH), F32)(
        pair_act, gain_in, bias_in, proj_in[:, 4 * CH :], proj_bias[None, 4 * CH :]
    )
    triangle = triangle.reshape(CH, 2, BLOCK // 2)
    triangle = lax.all_to_all(triangle, CHIPS, 0, 0, tiled=True).reshape(CH, BLOCK)
    return call(finish_kernel, (SIDE, SIDE, CH), F32)(
        triangle, gate, norm_out_gain[:, None], norm_out_bias[:, None], proj_out, out_bias[None]
    )


def solution(mesh):
    fine = Mesh(mesh.devices.reshape(2, 4, 2, 8, 2), ROW + COL)
    return jax.shard_map(
        body,
        mesh=fine,
        in_specs=(P(ROW, COL, None), P(), P(), P(), P(), P(), P(), P(), P(), P()),
        out_specs=P(ROW, COL, None),
        check_vma=False,
    )
```

```python
import jax
import jax.numpy as jnp
from jax import lax
from jax.experimental import pallas as pl
from jax.experimental.pallas import tpu as pltpu
from jax.sharding import Mesh
from jax.sharding import PartitionSpec as P

CH = 128
ROW = ("y_lo", "x", "core")
COL = ("z", "y_hi")
CHIPS = ("y_hi", "z", "y_lo", "x")
SWAP = [(0, 1), (1, 0)]
LANES = 128
SIDE = 48
HALF = SIDE // 2
WIDE = 32
THIN = 16
BLOCK = SIDE * SIDE
SHARE = BLOCK // 2
PIECE = 3 * LANES
F32 = jnp.float32
BF16 = jnp.bfloat16
EPS = 1e-05


def cat(parts, axis):
    return jnp.concatenate(list(parts), axis=axis)


def pieces(residues):
    for width, lo in ((WIDE, 0), (THIN, WIDE)):
        count = LANES // width
        n = residues // count
        for v in range(0, n, 3):
            yield [(b * n + u, lo, width) for u in range(v, v + 3) for b in range(count)]


def sides_kernel(
    act_hbm, mask_hbm, gain_hbm, bias_hbm, w_hbm, wb_hbm,
    out_ref, normed_ref,
    act, mask_v, gain_v, bias_v, w, wb, wt, wbt, sem,
):
    halves = [
        pltpu.make_async_copy(
            act_hbm.at[h * HALF : (h + 1) * HALF], act.at[h * HALF : (h + 1) * HALF], sem.at[h]
        )
        for h in range(2)
    ]
    small = [
        pltpu.make_async_copy(src, dst, sem.at[2 + n])
        for n, (src, dst) in enumerate(
            ((mask_hbm, mask_v), (gain_hbm, gain_v), (bias_hbm, bias_v), (w_hbm, w), (wb_hbm, wb))
        )
    ]
    for copy in halves[:1] + small + halves[1:]:
        copy.start()
    for copy in small:
        copy.wait()
    wt[...] = w[:, : 4 * CH].T
    for n in range(4):
        wbt[n * CH : (n + 1) * CH] = jnp.broadcast_to(wb[:, n * CH : (n + 1) * CH], (CH, LANES)).T
    total = mask_v.shape[1]
    known = jnp.broadcast_to(mask_v[...].astype(F32), (8, total))
    index = lax.broadcasted_iota(jnp.int32, (total, LANES), 0)
    place = lax.broadcasted_iota(jnp.int32, (total, LANES), 1)
    of_axis = []
    for axis in (ROW, COL):
        chosen = index == place + lax.axis_index(axis) * SIDE
        of_axis.append(jnp.dot(known, chosen.astype(F32), preferred_element_type=F32))
    row_mask, col_mask = of_axis
    index = lax.broadcasted_iota(jnp.int32, (LANES, PIECE), 0)
    place = lax.broadcasted_iota(jnp.int32, (LANES, PIECE), 1)
    for h in range(2):
        halves[h].wait()
        for at in range(h * HALF, (h + 1) * HALF, 8):
            values = act[at : at + 8].reshape(8 * SIDE, LANES)
            off = values - jnp.mean(values, axis=-1, keepdims=True)
            spread = jnp.mean(jnp.square(off), axis=-1, keepdims=True)
            normed = off * lax.rsqrt(spread + EPS) * gain_v[...] + bias_v[...]
            normed_ref[at : at + 8] = normed.astype(BF16).reshape(8, SIDE, LANES)
        for n, piece in enumerate(pieces(HALF)):
            rows = cat((normed_ref[h * HALF + k, lo : lo + width] for k, lo, width in piece), 0)
            _, lo, width = piece[0]
            count = LANES // width
            step = HALF // count
            k_of = h * HALF + piece[0][0] + place // LANES + (place % LANES) // width * step
            mask = jnp.dot(row_mask, (index == k_of).astype(F32), preferred_element_type=F32)
            i_of = lo + place % width
            mask = mask * jnp.dot(col_mask, (index == i_of).astype(F32), preferred_element_type=F32)
            for side in range(2):
                at = side * 2 * CH
                both = lax.dot_general(
                    wt[at : at + 2 * CH],
                    rows,
                    (((1,), (1,)), ((), ())),
                    preferred_element_type=F32,
                ) + wbt[at : at + 2 * CH, :1]
                value = mask[:1] * jax.nn.sigmoid(both[:CH]) * both[CH:]
                out_ref[side, h, :, n * PIECE : (n + 1) * PIECE] = value.astype(BF16)


def beside_kernel(normed_ref, w_ref, wb_ref, gate_ref, wide_ref, thin_ref):
    for n, piece in enumerate(pieces(SIDE)):
        rows = cat((normed_ref[k, lo : lo + width] for k, lo, width in piece), 0)
        lin = jnp.dot(rows, w_ref[...], preferred_element_type=F32) + wb_ref[...]
        gate_ref[n * PIECE : (n + 1) * PIECE] = jax.nn.sigmoid(lin)
    for ref, width in ((wide_ref, WIDE), (thin_ref, THIN)):
        count = LANES // width
        size = count * LANES
        lane = lax.broadcasted_iota(jnp.int32, (LANES, size), 1)
        row = lax.broadcasted_iota(jnp.int32, (LANES, 1), 0)
        for g in range(count):
            goes = (row // width * count + g) * width + row % width
            ref[g * LANES : (g + 1) * LANES] = (lane == goes).astype(F32).astype(BF16)


def gather_k(values, blocks, wide, thin, dst_ref, at):
    for width, perm, lanes_at, col_at in (
        (WIDE, wide, 0, 0),
        (THIN, thin, HALF * WIDE, blocks * WIDE),
    ):
        count = LANES // width
        n = HALF // count
        groups = blocks // count
        left = cat(
            (
                cat(
                    (
                        values[
                            (m * count + g) * 16 : (m * count + g + 1) * 16,
                            lanes_at + a * LANES : lanes_at + (a + 1) * LANES,
                        ]
                        for g in range(count)
                    ),
                    1,
                )
                for m in range(groups)
                for a in range(n)
            ),
            0,
        )
        moved = jnp.dot(left, perm[...], preferred_element_type=F32).astype(BF16)
        for m in range(groups):
            for b in range(count):
                dst_ref[
                    at + b * n * 16 : at + (b + 1) * n * 16,
                    col_at + m * LANES : col_at + (m + 1) * LANES,
                ] = moved[m * n * 16 : (m + 1) * n * 16, b * LANES : (b + 1) * LANES]


def triangle_kernel(mine_ref, got_ref, wide, thin, out_ref, left_ref, right_ref, tri_ref):
    start = pl.multiple_of(lax.axis_index("core") * CH, CH)
    for n, ref in enumerate((mine_ref, got_ref)):
        at = n * HALF * 16
        gather_k(ref[0, pl.ds(start, CH), :], 8, wide, thin, left_ref, at)
        gather_k(ref[1], 16, wide, thin, right_ref, at)
    product = lax.dot_general(
        left_ref[...], right_ref[...], (((0,), (0,)), ((), ())), preferred_element_type=F32
    )
    for strip in range(6):
        tri_ref[strip] = product[:, strip * LANES : (strip + 1) * LANES]

    def residue(strip, i):
        if i < WIDE:
            return tri_ref[strip, pl.ds(i, 8, stride=WIDE), :]
        return tri_ref[strip, pl.ds(8 * WIDE + i - WIDE, 8, stride=THIN), :]

    for width, perm, lanes_at, strip_at in (
        (WIDE, wide, 0, 0),
        (THIN, thin, SIDE * WIDE, 4),
    ):
        count = LANES // width
        n = SIDE // count
        groups = 16 // count
        left = cat(
            (
                cat((residue(strip_at + m, b * n + a) for b in range(count)), 1)
                for m in range(groups)
                for a in range(n)
            ),
            0,
        ).astype(BF16)
        moved = jnp.dot(left, perm[...], preferred_element_type=F32)
        for m in range(groups):
            for a in range(n):
                rows = moved[(m * n + a) * 8 : (m * n + a + 1) * 8]
                for g in range(0, count, 2):
                    at = (m * count + g) * 8
                    out_ref[
                        at : at + 16, lanes_at + a * LANES : lanes_at + (a + 1) * LANES
                    ] = cat(
                        (rows[:, g * LANES : (g + 1) * LANES], rows[:, (g + 1) * LANES : (g + 2) * LANES]), 0
                    ).astype(BF16)


def finish_kernel(tri_ref, gate_ref, gain_ref, bias_ref, w_ref, wb_ref, out_ref):
    twice = cat((w_ref[...], w_ref[...]), 0)
    for n, piece in enumerate(pieces(SIDE)):
        tri = tri_ref[:, n * PIECE : (n + 1) * PIECE].astype(F32)
        off = tri - jnp.mean(tri, axis=0, keepdims=True)
        spread = jnp.mean(jnp.square(off), axis=0, keepdims=True)
        mixed = off * lax.rsqrt(spread + EPS) * gain_ref[...] + bias_ref[...]
        high = mixed.astype(BF16)
        low = (mixed - high.astype(F32)).astype(BF16)
        lin = lax.dot_general(
            cat((high, low), 0), twice, (((0,), (0,)), ((), ())), preferred_element_type=F32
        )
        update = gate_ref[n * PIECE : (n + 1) * PIECE] * (lin + wb_ref[...])
        at = 0
        for i, lo, width in piece:
            out_ref[i, lo : lo + width] = update[at : at + width]
            at += width


def call(kernel, outs, scratch=(), in_specs=None, cost=10**9):
    options = {} if in_specs is None else {"in_specs": in_specs}
    return pl.pallas_call(
        kernel,
        out_shape=outs,
        scratch_shapes=scratch,
        compiler_params=pltpu.CompilerParams(vmem_limit_bytes=40 * 2**20),
        cost_estimate=pl.CostEstimate(flops=cost, bytes_accessed=3 * 10**6, transcendentals=0),
        **options,
    )


def body(
    pair_act,
    residue_mask,
    norm_in_gain,
    norm_in_bias,
    proj_in,
    proj_bias,
    norm_out_gain,
    norm_out_bias,
    proj_out,
    out_bias,
):
    shape = jax.ShapeDtypeStruct
    vmem = pltpu.VMEM
    total = residue_mask.shape[0]
    sides, normed = call(
        sides_kernel,
        (shape((2, 2, CH, SHARE), BF16), shape((SIDE, SIDE, CH), BF16)),
        [
            vmem((SIDE, SIDE, CH), F32),
            vmem((1, total), jnp.int32),
            vmem((1, CH), F32),
            vmem((1, CH), F32),
            vmem((CH, 5 * CH), BF16),
            vmem((1, 5 * CH), F32),
            vmem((4 * CH, CH), BF16),
            vmem((4 * CH, LANES), F32),
            pltpu.SemaphoreType.DMA((7,)),
        ],
        [pl.BlockSpec(memory_space=pltpu.HBM)] * 6,
    )(
        pair_act,
        residue_mask[None],
        norm_in_gain[None],
        norm_in_bias[None],
        proj_in,
        proj_bias[None],
    )
    packed = sides.transpose(2, 1, 0, 3).reshape(2 * CH, 2, SHARE)
    packed = lax.all_to_all(packed, CHIPS + ("core",), 0, 0, tiled=True)
    gate, wide, thin = call(
        beside_kernel,
        (shape((BLOCK, CH), F32), shape((512, 512), BF16), shape((1024, 1024), BF16)),
    )(normed, proj_in[:, 4 * CH :], proj_bias[None, 4 * CH :])
    mine = packed.transpose(1, 0, 2)
    got = lax.ppermute(mine, "core", SWAP)
    triangle = call(
        triangle_kernel,
        shape((CH, BLOCK), BF16),
        [
            vmem((16 * SIDE, 8 * SIDE), BF16),
            vmem((16 * SIDE, 16 * SIDE), BF16),
            vmem((6, 8 * SIDE, LANES), F32),
        ],
    )(mine, got, wide, thin)
    triangle = triangle.reshape(CH, 2, BLOCK // 2)
    triangle = lax.all_to_all(triangle, CHIPS, 0, 0, tiled=True).reshape(CH, BLOCK)
    return call(finish_kernel, shape((SIDE, SIDE, CH), F32))(
        triangle, gate, norm_out_gain[:, None], norm_out_bias[:, None], proj_out, out_bias[None]
    )


def solution(mesh):
    fine = Mesh(mesh.devices.reshape(2, 4, 2, 8, 2), ROW + COL)
    return jax.shard_map(
        body,
        mesh=fine,
        in_specs=(P(ROW, COL, None), P(), P(), P(), P(), P(), P(), P(), P(), P()),
        out_specs=P(ROW, COL, None),
        check_vma=False,
    )
```

```python
import jax
import jax.numpy as jnp
from jax import lax
from jax.experimental import pallas as pl
from jax.experimental.pallas import tpu as pltpu
from jax.sharding import Mesh
from jax.sharding import PartitionSpec as P

CH = 128
ROW = ("y_lo", "x", "core")
COL = ("z", "y_hi")
CHIPS = ("y_hi", "z", "y_lo", "x")
SWAP = [(0, 1), (1, 0)]
LANES = 128
SIDE = 48
HALF = SIDE // 2
WIDE = 32
THIN = 16
BLOCK = SIDE * SIDE
SHARE = BLOCK // 2
PIECE = 3 * LANES
F32 = jnp.float32
BF16 = jnp.bfloat16
EPS = 1e-05


def cat(parts, axis):
    return jnp.concatenate(list(parts), axis=axis)


def pieces(residues):
    for width, lo in ((WIDE, 0), (THIN, WIDE)):
        count = LANES // width
        n = residues // count
        for v in range(0, n, 3):
            yield [(b * n + u, lo, width) for u in range(v, v + 3) for b in range(count)]


def sides_kernel(
    act_hbm, mask_hbm, gain_hbm, bias_hbm, w_hbm, wb_hbm,
    out_ref, normed_ref, gate_w_ref, gate_b_ref,
    act, mask_v, gain_v, bias_v, w, wb, wt, wbt, sem,
):
    halves = [
        pltpu.make_async_copy(
            act_hbm.at[h * HALF : (h + 1) * HALF], act.at[h * HALF : (h + 1) * HALF], sem.at[h]
        )
        for h in range(2)
    ]
    small = [
        pltpu.make_async_copy(src, dst, sem.at[2 + n])
        for n, (src, dst) in enumerate(
            ((mask_hbm, mask_v.at[0]), (gain_hbm, gain_v.at[0]), (bias_hbm, bias_v.at[0]), (w_hbm, w), (wb_hbm, wb.at[0]))
        )
    ]
    for copy in halves[:1] + small + halves[1:]:
        copy.start()
    for copy in small:
        copy.wait()
    wt[...] = w[:, : 4 * CH].T
    gate_w_ref[...] = w[:, 4 * CH :]
    gate_b_ref[...] = jnp.broadcast_to(wb[:, 4 * CH :], gate_b_ref.shape)
    for n in range(4):
        wbt[n * CH : (n + 1) * CH] = jnp.broadcast_to(wb[:, n * CH : (n + 1) * CH], (CH, LANES)).T
    total = mask_v.shape[1]
    known = jnp.broadcast_to(mask_v[...].astype(F32), (8, total))
    index = lax.broadcasted_iota(jnp.int32, (total, LANES), 0)
    place = lax.broadcasted_iota(jnp.int32, (total, LANES), 1)
    of_axis = []
    for axis in (ROW, COL):
        chosen = index == place + lax.axis_index(axis) * SIDE
        of_axis.append(jnp.dot(known, chosen.astype(F32), preferred_element_type=F32))
    row_mask, col_mask = of_axis
    index = lax.broadcasted_iota(jnp.int32, (LANES, PIECE), 0)
    place = lax.broadcasted_iota(jnp.int32, (LANES, PIECE), 1)
    for h in range(2):
        halves[h].wait()
        for at in range(h * HALF, (h + 1) * HALF, 8):
            values = act[at : at + 8].reshape(8 * SIDE, LANES)
            off = values - jnp.mean(values, axis=-1, keepdims=True)
            spread = jnp.mean(jnp.square(off), axis=-1, keepdims=True)
            normed = off * lax.rsqrt(spread + EPS) * gain_v[...] + bias_v[...]
            normed_ref[at : at + 8] = normed.astype(BF16).reshape(8, SIDE, LANES)
        for n, piece in enumerate(pieces(HALF)):
            rows = cat((normed_ref[h * HALF + k, lo : lo + width] for k, lo, width in piece), 0)
            _, lo, width = piece[0]
            count = LANES // width
            step = HALF // count
            k_of = h * HALF + piece[0][0] + place // LANES + (place % LANES) // width * step
            mask = jnp.dot(row_mask, (index == k_of).astype(F32), preferred_element_type=F32)
            i_of = lo + place % width
            mask = mask * jnp.dot(col_mask, (index == i_of).astype(F32), preferred_element_type=F32)
            for side in range(2):
                at = side * 2 * CH
                both = lax.dot_general(
                    wt[at : at + 2 * CH],
                    rows,
                    (((1,), (1,)), ((), ())),
                    preferred_element_type=F32,
                ) + wbt[at : at + 2 * CH, :1]
                value = mask[:1] * jax.nn.sigmoid(both[:CH]) * both[CH:]
                out_ref[side, h, :, n * PIECE : (n + 1) * PIECE] = value.astype(BF16)


def gather_k(values, blocks, wide, thin, dst_ref, at):
    for width, perm, lanes_at, col_at in (
        (WIDE, wide, 0, 0),
        (THIN, thin, HALF * WIDE, blocks * WIDE),
    ):
        count = LANES // width
        n = HALF // count
        groups = blocks // count
        left = cat(
            (
                cat(
                    (
                        values[
                            (m * count + g) * 16 : (m * count + g + 1) * 16,
                            lanes_at + a * LANES : lanes_at + (a + 1) * LANES,
                        ]
                        for g in range(count)
                    ),
                    1,
                )
                for m in range(groups)
                for a in range(n)
            ),
            0,
        )
        moved = jnp.dot(left, perm[...], preferred_element_type=F32).astype(BF16)
        for m in range(groups):
            for b in range(count):
                dst_ref[
                    at + b * n * 16 : at + (b + 1) * n * 16,
                    col_at + m * LANES : col_at + (m + 1) * LANES,
                ] = moved[m * n * 16 : (m + 1) * n * 16, b * LANES : (b + 1) * LANES]


def gather_sides(ref, wide, thin, left_ref, right_ref, at):
    start = pl.multiple_of(lax.axis_index("core") * CH, CH)
    gather_k(ref[0, pl.ds(start, CH), :], 8, wide, thin, left_ref, at)
    gather_k(ref[1], 16, wide, thin, right_ref, at)


def build_permutations(wide_ref, thin_ref):
    for ref, width in ((wide_ref, WIDE), (thin_ref, THIN)):
        count = LANES // width
        size = count * LANES
        lane = lax.broadcasted_iota(jnp.int32, (LANES, size), 1)
        row = lax.broadcasted_iota(jnp.int32, (LANES, 1), 0)
        for g in range(count):
            goes = (row // width * count + g) * width + row % width
            ref[g * LANES : (g + 1) * LANES] = (lane == goes).astype(F32).astype(BF16)


def beside_kernel(
    mine_ref, normed_ref, w_ref, wb_ref, gain_hbm, bias_hbm, out_w_hbm, out_b_hbm,
    left_ref, right_ref, gate_ref, wide_ref, thin_ref, gain_ref, bias_ref, twice_ref, out_b_ref,
    gain_v, bias_v, out_b_v, sem,
):
    copies = [
        pltpu.make_async_copy(src, dst, sem.at[n])
        for n, (src, dst) in enumerate(
            (
                (gain_hbm, gain_v.at[0]),
                (bias_hbm, bias_v.at[0]),
                (out_b_hbm, out_b_v.at[0]),
                (out_w_hbm, twice_ref.at[:CH]),
                (out_w_hbm, twice_ref.at[CH:]),
            )
        )
    ]
    for copy in copies:
        copy.start()
    build_permutations(wide_ref, thin_ref)
    gather_sides(mine_ref, wide_ref, thin_ref, left_ref, right_ref, 0)
    for n, piece in enumerate(pieces(SIDE)):
        rows = cat((normed_ref[k, lo : lo + width] for k, lo, width in piece), 0)
        lin = jnp.dot(rows, w_ref[...], preferred_element_type=F32) + wb_ref[:1]
        gate_ref[n * PIECE : (n + 1) * PIECE] = jax.nn.sigmoid(lin)
    for copy in copies:
        copy.wait()
    gain_ref[...] = jnp.broadcast_to(gain_v[...], (CH, LANES)).T
    bias_ref[...] = jnp.broadcast_to(bias_v[...], (CH, LANES)).T
    out_b_ref[...] = jnp.broadcast_to(out_b_v[...], out_b_ref.shape)


def triangle_kernel(
    left_mine, right_mine, got_ref, wide, thin, out_ref, left_ref, right_ref, tri_ref
):
    own = HALF * 16
    left_ref[:own] = left_mine[...]
    right_ref[:own] = right_mine[...]
    gather_sides(got_ref, wide, thin, left_ref, right_ref, own)
    product = lax.dot_general(
        left_ref[...], right_ref[...], (((0,), (0,)), ((), ())), preferred_element_type=F32
    )
    for strip in range(6):
        tri_ref[strip] = product[:, strip * LANES : (strip + 1) * LANES]

    def residue(strip, i):
        if i < WIDE:
            return tri_ref[strip, pl.ds(i, 8, stride=WIDE), :]
        return tri_ref[strip, pl.ds(8 * WIDE + i - WIDE, 8, stride=THIN), :]

    for width, perm, lanes_at, strip_at in (
        (WIDE, wide, 0, 0),
        (THIN, thin, SIDE * WIDE, 4),
    ):
        count = LANES // width
        n = SIDE // count
        groups = 16 // count
        left = cat(
            (
                cat((residue(strip_at + m, b * n + a) for b in range(count)), 1)
                for m in range(groups)
                for a in range(n)
            ),
            0,
        ).astype(BF16)
        moved = jnp.dot(left, perm[...], preferred_element_type=F32)
        for m in range(groups):
            for a in range(n):
                rows = moved[(m * n + a) * 8 : (m * n + a + 1) * 8]
                for g in range(0, count, 2):
                    at = (m * count + g) * 8
                    two = cat(
                        (rows[:, (g + d) * LANES : (g + d + 1) * LANES] for d in range(2)), 0
                    )
                    half, lane = divmod(lanes_at + a * LANES, SHARE)
                    out_ref[half, at : at + 16, lane : lane + LANES] = two.astype(BF16)


def finish_kernel(tri_ref, gate_ref, gain_ref, bias_ref, twice_ref, wb_ref, out_hbm, out, sem):
    copies = []
    for n, piece in enumerate(pieces(SIDE)):
        half, lane = divmod(n * PIECE, SHARE)
        tri = tri_ref[half, :, lane : lane + PIECE].astype(F32)
        off = tri - jnp.mean(tri, axis=0, keepdims=True)
        spread = jnp.mean(jnp.square(off), axis=0, keepdims=True)
        mixed = off * lax.rsqrt(spread + EPS) * gain_ref[:, :1] + bias_ref[:, :1]
        high = mixed.astype(BF16)
        low = (mixed - high.astype(F32)).astype(BF16)
        lin = lax.dot_general(
            cat((high, low), 0),
            twice_ref[...],
            (((0,), (0,)), ((), ())),
            preferred_element_type=F32,
        )
        update = gate_ref[n * PIECE : (n + 1) * PIECE] * (lin + wb_ref[:1])
        for at, (i, lo, width) in enumerate(piece):
            out[i, lo : lo + width] = update[at * width : (at + 1) * width]
        count = len(piece) // 3
        for i, lo, width in piece[:count]:
            where = (slice(i, i + 3), slice(lo, lo + width))
            copy = pltpu.make_async_copy(out.at[where], out_hbm.at[where], sem.at[len(copies)])
            copy.start()
            copies.append(copy)
    for copy in copies:
        copy.wait()


def call(kernel, outs, scratch=(), cost=10**9, **options):
    return pl.pallas_call(
        kernel,
        out_shape=outs,
        scratch_shapes=scratch,
        compiler_params=pltpu.CompilerParams(vmem_limit_bytes=40 * 2**20),
        cost_estimate=pl.CostEstimate(flops=cost, bytes_accessed=3 * 10**6, transcendentals=0),
        **options,
    )


def stay(arrays):
    return [pltpu.with_memory_space_constraint(x, pltpu.HBM) for x in arrays]


def body(
    pair_act,
    residue_mask,
    norm_in_gain,
    norm_in_bias,
    proj_in,
    proj_bias,
    norm_out_gain,
    norm_out_bias,
    proj_out,
    out_bias,
):
    shape = jax.ShapeDtypeStruct
    vmem = pltpu.VMEM
    total = residue_mask.shape[0]
    hbm, here = pl.BlockSpec(memory_space=pltpu.HBM), pl.BlockSpec(memory_space=vmem)
    sides, normed, gate_w, gate_b = call(
        sides_kernel,
        (
            shape((2, 2, CH, SHARE), BF16),
            shape((SIDE, SIDE, CH), BF16),
            shape((CH, CH), BF16),
            shape((8, CH), F32),
        ),
        [
            vmem((SIDE, SIDE, CH), F32),
            vmem((1, total), jnp.int32),
            vmem((1, CH), F32),
            vmem((1, CH), F32),
            vmem((CH, 5 * CH), BF16),
            vmem((1, 5 * CH), F32),
            vmem((4 * CH, CH), BF16),
            vmem((4 * CH, LANES), F32),
            pltpu.SemaphoreType.DMA((7,)),
        ],
        in_specs=[hbm] * 6,
    )(*stay((pair_act, residue_mask, norm_in_gain, norm_in_bias, proj_in, proj_bias)))
    packed = sides.transpose(2, 1, 0, 3).reshape(2 * CH, 2, SHARE)
    packed = lax.all_to_all(packed, CHIPS + ("core",), 0, 0, tiled=True)
    mine = packed.transpose(1, 0, 2)
    got = lax.ppermute(mine, "core", SWAP)
    left, right, gate, wide, thin, *last = call(
        beside_kernel,
        (
            shape((8 * SIDE, 8 * SIDE), BF16),
            shape((8 * SIDE, 16 * SIDE), BF16),
            shape((BLOCK, CH), F32),
            shape((512, 512), BF16),
            shape((1024, 1024), BF16),
            shape((CH, LANES), F32),
            shape((CH, LANES), F32),
            shape((2 * CH, CH), BF16),
            shape((8, CH), F32),
        ),
        [vmem((1, CH), F32)] * 3 + [pltpu.SemaphoreType.DMA((5,))],
        in_specs=[here] * 4 + [hbm] * 4,
    )(mine, normed, gate_w, gate_b, *stay((norm_out_gain, norm_out_bias, proj_out, out_bias)))
    triangle = call(
        triangle_kernel,
        shape((2, CH, SHARE), BF16),
        [
            vmem((16 * SIDE, 8 * SIDE), BF16),
            vmem((16 * SIDE, 16 * SIDE), BF16),
            vmem((6, 8 * SIDE, LANES), F32),
        ],
    )(left, right, got, wide, thin)
    triangle = lax.all_to_all(triangle.transpose(1, 0, 2), CHIPS, 0, 0, tiled=True)
    return call(
        finish_kernel,
        shape((SIDE, SIDE, CH), F32),
        [vmem((SIDE, SIDE, CH), F32), pltpu.SemaphoreType.DMA((32,))],
        out_specs=hbm,
    )(triangle.transpose(1, 0, 2), gate, *last)


def solution(mesh):
    fine = Mesh(mesh.devices.reshape(2, 4, 2, 8, 2), ROW + COL)
    return jax.shard_map(
        body,
        mesh=fine,
        in_specs=(P(ROW, COL, None), P(), P(), P(), P(), P(), P(), P(), P(), P()),
        out_specs=P(ROW, COL, None),
        check_vma=False,
    )
```

```python
import jax
import jax.numpy as jnp
from jax import lax
from jax.experimental import pallas as pl
from jax.experimental.pallas import tpu as pltpu
from jax.sharding import Mesh
from jax.sharding import PartitionSpec as P

CH = 128
ROW = ("y_lo", "x", "core")
COL = ("z", "y_hi")
ALL = ROW + COL
TURN = (3, 6, 0, 5, 1, 7, 2, 4)
HALVES = (1, 0)
SWAP = [(0, 1), (1, 0)]
LANES = 128
SIDE = 48
HALF = SIDE // 2
WIDE = 32
THIN = 16
BLOCK = SIDE * SIDE
SHARE = BLOCK // 2
PIECE = 3 * LANES
F32 = jnp.float32
BF16 = jnp.bfloat16
EPS = 1e-05


def cat(parts, axis):
    return jnp.concatenate(list(parts), axis=axis)


def pieces(residues):
    for width, lo in ((WIDE, 0), (THIN, WIDE)):
        count = LANES // width
        n = residues // count
        for v in range(0, n, 3):
            yield [(b * n + u, lo, width) for u in range(v, v + 3) for b in range(count)]


def sides_kernel(
    act_hbm, mask_hbm, gain_hbm, bias_hbm, w_hbm, wb_hbm,
    out_ref, normed_ref, gate_w_ref, gate_b_ref,
    act, mask_v, gain_v, bias_v, w, wb, wt32, wt, wbt, sem,
):
    halves = [
        pltpu.make_async_copy(
            act_hbm.at[h * HALF : (h + 1) * HALF], act.at[h * HALF : (h + 1) * HALF], sem.at[h]
        )
        for h in range(2)
    ]
    small = [
        pltpu.make_async_copy(src, dst, sem.at[2 + n])
        for n, (src, dst) in enumerate(
            ((mask_hbm, mask_v.at[0]), (gain_hbm, gain_v.at[0]), (bias_hbm, bias_v.at[0]), (w_hbm, w), (wb_hbm, wb.at[0]))
        )
    ]
    for copy in halves[:1] + small + halves[1:]:
        copy.start()
    for copy in small:
        copy.wait()
    for n in range(4):
        side, kind = divmod(n, 2)
        cols = slice(n * CH, (n + 1) * CH)
        rows = pl.ds(kind * 2 * CH + side, CH, stride=2)
        wt32[rows, :] = w[:, cols].astype(F32).T
        wbt[rows, :] = jnp.broadcast_to(wb[:, cols], (CH, LANES)).T
    wt[...] = wt32[...].astype(BF16)
    gate_w_ref[...] = w[:, 4 * CH :]
    gate_b_ref[...] = jnp.broadcast_to(wb[:, 4 * CH :], gate_b_ref.shape)
    total = mask_v.shape[1]
    known = jnp.broadcast_to(mask_v[...].astype(F32), (8, total))
    index = lax.broadcasted_iota(jnp.int32, (total, LANES), 0)
    place = lax.broadcasted_iota(jnp.int32, (total, LANES), 1)
    of_axis = []
    for axis in (ROW, COL):
        chosen = index == place + lax.axis_index(axis) * SIDE
        of_axis.append(jnp.dot(known, chosen.astype(F32), preferred_element_type=F32))
    row_mask, col_mask = of_axis
    index = lax.broadcasted_iota(jnp.int32, (LANES, PIECE), 0)
    place = lax.broadcasted_iota(jnp.int32, (LANES, PIECE), 1)
    for h in range(2):
        halves[h].wait()
        for at in range(h * HALF, (h + 1) * HALF, 8):
            values = act[at : at + 8].reshape(8 * SIDE, LANES)
            off = values - jnp.mean(values, axis=-1, keepdims=True)
            spread = jnp.mean(jnp.square(off), axis=-1, keepdims=True)
            normed = off * lax.rsqrt(spread + EPS) * gain_v[...] + bias_v[...]
            normed_ref[at : at + 8] = normed.astype(BF16).reshape(8, SIDE, LANES)
    for n, piece in enumerate(pieces(SIDE)):
        rows = cat((normed_ref[k, lo : lo + width] for k, lo, width in piece), 0)
        _, lo, width = piece[0]
        step = SIDE * width // LANES
        k_of = piece[0][0] + place // LANES + (place % LANES) // width * step
        mask = jnp.dot(row_mask, (index == k_of).astype(F32), preferred_element_type=F32)
        i_of = lo + place % width
        mask = mask * jnp.dot(col_mask, (index == i_of).astype(F32), preferred_element_type=F32)
        gate, value = (
            lax.dot_general(
                wt[at : at + 2 * CH],
                rows,
                (((1,), (1,)), ((), ())),
                preferred_element_type=F32,
            )
            + wbt[at : at + 2 * CH, :1]
            for at in (0, 2 * CH)
        )
        value = mask[:1] * jax.nn.sigmoid(gate) * value
        out_ref[:, n * PIECE : (n + 1) * PIECE] = value.astype(BF16)


def gather_k(values, blocks, wide, thin, dst_ref):
    for width, perm, lanes_at, col_at in (
        (WIDE, wide, 0, 0),
        (THIN, thin, SIDE * WIDE, blocks * WIDE),
    ):
        count = LANES // width
        n = SIDE // count
        groups = blocks // count
        left = cat(
            (
                cat(
                    (
                        values[
                            (m * count + g) * 8 : (m * count + g + 1) * 8,
                            lanes_at + a * LANES : lanes_at + (a + 1) * LANES,
                        ]
                        for g in range(count)
                    ),
                    1,
                )
                for m in range(groups)
                for a in range(n)
            ),
            0,
        ).astype(BF16)
        moved = jnp.dot(left, perm[...], preferred_element_type=F32).astype(BF16)
        for m in range(groups):
            for b in range(count):
                dst_ref[
                    b * n * 8 : (b + 1) * n * 8,
                    col_at + m * LANES : col_at + (m + 1) * LANES,
                ] = moved[m * n * 8 : (m + 1) * n * 8, b * LANES : (b + 1) * LANES]


def product(ref, wide, thin, left_ref, right_ref):
    core, half = lax.axis_index("core"), CH // 2
    start = pl.multiple_of((core if HALVES[0] == 0 else 1 - core) * half, half)
    gather_k(ref[0, pl.ds(start, half), :].astype(F32), 8, wide, thin, left_ref)
    gather_k(ref[1].astype(F32), 16, wide, thin, right_ref)
    return lax.dot_general(
        left_ref[...], right_ref[...], (((0,), (0,)), ((), ())), preferred_element_type=F32
    )


def build_permutations(wide_ref, thin_ref):
    for ref, width in ((wide_ref, WIDE), (thin_ref, THIN)):
        count = LANES // width
        size = count * LANES
        lane = lax.broadcasted_iota(jnp.int32, (LANES, size), 1)
        row = lax.broadcasted_iota(jnp.int32, (LANES, 1), 0)
        for g in range(count):
            goes = (row // width * count + g) * width + row % width
            ref[g * LANES : (g + 1) * LANES] = (lane == goes).astype(F32).astype(BF16)


def beside_kernel(
    mine_ref, normed_ref, w_ref, wb_ref, gain_hbm, bias_hbm, out_w_hbm, out_b_hbm,
    part_ref, gate_ref, wide_ref, thin_ref, gain_ref, bias_ref, twice_ref, out_b_ref,
    left_ref, right_ref, gain_v, bias_v, out_b_v, sem,
):
    copies = [
        pltpu.make_async_copy(src, dst, sem.at[n])
        for n, (src, dst) in enumerate(
            (
                (gain_hbm, gain_v.at[0]),
                (bias_hbm, bias_v.at[0]),
                (out_b_hbm, out_b_v.at[0]),
                (out_w_hbm, twice_ref.at[:CH]),
                (out_w_hbm, twice_ref.at[CH:]),
            )
        )
    ]
    for copy in copies:
        copy.start()
    build_permutations(wide_ref, thin_ref)
    part_ref[...] = product(mine_ref, wide_ref, thin_ref, left_ref, right_ref)
    for n, piece in enumerate(pieces(SIDE)):
        rows = cat((normed_ref[k, lo : lo + width] for k, lo, width in piece), 0)
        lin = jnp.dot(rows, w_ref[...], preferred_element_type=F32) + wb_ref[:1]
        gate_ref[n * PIECE : (n + 1) * PIECE] = jax.nn.sigmoid(lin)
    for copy in copies:
        copy.wait()
    gain_ref[...] = jnp.broadcast_to(gain_v[...], (CH, LANES)).T
    bias_ref[...] = jnp.broadcast_to(bias_v[...], (CH, LANES)).T
    out_b_ref[...] = jnp.broadcast_to(out_b_v[...], out_b_ref.shape)


def triangle_kernel(part_ref, got_ref, wide, thin, out_ref, left_ref, right_ref, tri_ref, out):
    total = part_ref[...] + product(got_ref, wide, thin, left_ref, right_ref)
    for strip in range(6):
        tri_ref[strip] = total[:, strip * LANES : (strip + 1) * LANES]

    def residue(strip, i):
        if i < WIDE:
            return tri_ref[strip, pl.ds(i, 8, stride=WIDE), :]
        return tri_ref[strip, pl.ds(8 * WIDE + i - WIDE, 8, stride=THIN), :]

    for width, perm, lanes_at, strip_at in (
        (WIDE, wide, 0, 0),
        (THIN, thin, SIDE * WIDE, 4),
    ):
        count = LANES // width
        n = SIDE // count
        groups = 16 // count
        left = cat(
            (
                cat((residue(strip_at + m, b * n + a) for b in range(count)), 1)
                for m in range(groups)
                for a in range(n)
            ),
            0,
        ).astype(BF16)
        moved = jnp.dot(left, perm[...], preferred_element_type=F32)
        for m in range(groups):
            for a in range(n):
                rows = moved[(m * n + a) * 8 : (m * n + a + 1) * 8]
                half, lane = divmod(lanes_at + a * LANES, SHARE)
                for g in range(count):
                    to = pl.ds((m * count + g) * 16 + half, 8, stride=2)
                    out[lane // LANES, to, :] = rows[:, g * LANES : (g + 1) * LANES]
    for strip in range(SHARE // LANES):
        out_ref[:, strip * LANES : (strip + 1) * LANES] = out[strip].astype(BF16)


def finish_kernel(tri_ref, gate_ref, gain_ref, bias_ref, twice_ref, wb_ref, out_hbm, out, sem):
    copies = []
    for n, piece in enumerate(pieces(SIDE)):
        half, lane = divmod(n * PIECE, SHARE)
        tri = tri_ref[half, :, lane : lane + PIECE].astype(F32)
        off = tri - jnp.mean(tri, axis=0, keepdims=True)
        spread = jnp.mean(jnp.square(off), axis=0, keepdims=True)
        mixed = off * lax.rsqrt(spread + EPS) * gain_ref[:, :1] + bias_ref[:, :1]
        high = mixed.astype(BF16)
        low = (mixed - high.astype(F32)).astype(BF16)
        lin = lax.dot_general(
            cat((high, low), 0),
            twice_ref[...],
            (((0,), (0,)), ((), ())),
            preferred_element_type=F32,
        )
        update = gate_ref[n * PIECE : (n + 1) * PIECE] * (lin + wb_ref[:1])
        for at, (i, lo, width) in enumerate(piece):
            out[i, lo : lo + width] = update[at * width : (at + 1) * width]
        count = len(piece) // 3
        for i, lo, width in piece[:count]:
            where = (slice(i, i + 3), slice(lo, lo + width))
            copy = pltpu.make_async_copy(out.at[where], out_hbm.at[where], sem.at[len(copies)])
            copy.start()
            copies.append(copy)
    for copy in copies:
        copy.wait()


def call(kernel, outs, scratch=(), cost=10**9, **options):
    return pl.pallas_call(
        kernel,
        out_shape=outs,
        scratch_shapes=scratch,
        compiler_params=pltpu.CompilerParams(vmem_limit_bytes=40 * 2**20),
        cost_estimate=pl.CostEstimate(flops=cost, bytes_accessed=3 * 10**6, transcendentals=0),
        **options,
    )


def groups():
    chips = [
        [(pair * 2 + core) * 16 + z * 2 + y_hi for core in range(2)]
        for y_hi in HALVES
        for z in TURN
        for pair in TURN
    ]
    return [[chip[core] for chip in chips] for core in range(2)]


def stay(arrays):
    return [pltpu.with_memory_space_constraint(x, pltpu.HBM) for x in arrays]


def body(
    pair_act,
    residue_mask,
    norm_in_gain,
    norm_in_bias,
    proj_in,
    proj_bias,
    norm_out_gain,
    norm_out_bias,
    proj_out,
    out_bias,
):
    shape = jax.ShapeDtypeStruct
    vmem = pltpu.VMEM
    total = residue_mask.shape[0]
    hbm, here = pl.BlockSpec(memory_space=pltpu.HBM), pl.BlockSpec(memory_space=vmem)
    sides, normed, gate_w, gate_b = call(
        sides_kernel,
        (
            shape((2 * CH, BLOCK), BF16),
            shape((SIDE, SIDE, CH), BF16),
            shape((CH, CH), BF16),
            shape((8, CH), F32),
        ),
        [
            vmem((SIDE, SIDE, CH), F32),
            vmem((1, total), jnp.int32),
            vmem((1, CH), F32),
            vmem((1, CH), F32),
            vmem((CH, 5 * CH), BF16),
            vmem((1, 5 * CH), F32),
            vmem((4 * CH, CH), F32),
            vmem((4 * CH, CH), BF16),
            vmem((4 * CH, LANES), F32),
            pltpu.SemaphoreType.DMA((7,)),
        ],
        in_specs=[hbm] * 6,
    )(*stay((pair_act, residue_mask, norm_in_gain, norm_in_bias, proj_in, proj_bias)))
    packed = sides.reshape(CH, 2, BLOCK)
    packed = lax.all_to_all(packed, ALL, 0, 0, axis_index_groups=groups(), tiled=True)
    mine = packed.transpose(1, 0, 2)
    got = lax.ppermute(mine, "core", SWAP)
    operands = [vmem((8 * SIDE, 8 * SIDE), BF16), vmem((8 * SIDE, 16 * SIDE), BF16)]
    part, gate, wide, thin, *last = call(
        beside_kernel,
        (
            shape((8 * SIDE, 16 * SIDE), F32),
            shape((BLOCK, CH), F32),
            shape((512, 512), BF16),
            shape((1024, 1024), BF16),
            shape((CH, LANES), F32),
            shape((CH, LANES), F32),
            shape((2 * CH, CH), BF16),
            shape((8, CH), F32),
        ),
        [*operands, *[vmem((1, CH), F32)] * 3, pltpu.SemaphoreType.DMA((5,))],
        in_specs=[here] * 4 + [hbm] * 4,
    )(mine, normed, gate_w, gate_b, *stay((norm_out_gain, norm_out_bias, proj_out, out_bias)))
    triangle = call(
        triangle_kernel,
        shape((2 * CH, SHARE), BF16),
        [*operands, vmem((6, 8 * SIDE, LANES), F32), vmem((SHARE // LANES, 2 * CH, LANES), F32)],
    )(part, got, wide, thin)
    triangle = triangle.reshape(CH, 2, SHARE)
    triangle = lax.all_to_all(
        triangle, ALL, 0, 0, axis_index_groups=groups(), tiled=True
    )
    return call(
        finish_kernel,
        shape((SIDE, SIDE, CH), F32),
        [vmem((SIDE, SIDE, CH), F32), pltpu.SemaphoreType.DMA((32,))],
        out_specs=hbm,
    )(triangle.transpose(1, 0, 2), gate, *last)


def solution(mesh):
    fine = Mesh(mesh.devices.reshape(2, 4, 2, 8, 2), ROW + COL)
    return jax.shard_map(
        body,
        mesh=fine,
        in_specs=(P(ROW, COL, None), P(), P(), P(), P(), P(), P(), P(), P(), P()),
        out_specs=P(ROW, COL, None),
        check_vma=False,
    )
```

```python
import jax
import jax.numpy as jnp
from jax import lax
from jax.experimental import pallas as pl
from jax.experimental.pallas import tpu as pltpu
from jax.sharding import Mesh
from jax.sharding import PartitionSpec as P

CH = 128
ROW = ("y_lo", "x", "core")
COL = ("z", "y_hi")
ALL = ROW + COL
TURN = (6, 3, 1, 0, 7, 2, 5, 4)
PAIRS = (6, 3, 1, 0, 7, 2, 5, 4)
HALVES = (1, 0)
SWAP = [(0, 1), (1, 0)]
LANES = 128
SIDE = 48
HALF = SIDE // 2
WIDE = 32
THIN = 16
BLOCK = SIDE * SIDE
SHARE = BLOCK // 2
PIECE = 3 * LANES
F32 = jnp.float32
BF16 = jnp.bfloat16
EPS = 1e-05


def cat(parts, axis):
    return jnp.concatenate(list(parts), axis=axis)


def across(column):
    return cat([column] * (PIECE // LANES), 1)


def pieces(residues):
    for width, lo in ((WIDE, 0), (THIN, WIDE)):
        count = LANES // width
        n = residues // count
        for v in range(0, n, 3):
            yield [(b * n + u, lo, width) for u in range(v, v + 3) for b in range(count)]


def sides_kernel(
    act_hbm, mask_hbm, gain_hbm, bias_hbm, w_hbm, wb_hbm,
    out_ref, normed_ref, gate_w_ref, gate_b_ref,
    act, mask_v, gain_v, bias_v, w, wb, wt32, wt, wbt, sem,
):
    halves = [
        pltpu.make_async_copy(
            act_hbm.at[h * HALF : (h + 1) * HALF], act.at[h * HALF : (h + 1) * HALF], sem.at[h]
        )
        for h in range(2)
    ]
    small = [
        pltpu.make_async_copy(src, dst, sem.at[2 + n])
        for n, (src, dst) in enumerate(
            ((mask_hbm, mask_v.at[0]), (gain_hbm, gain_v.at[0]), (bias_hbm, bias_v.at[0]), (w_hbm, w), (wb_hbm, wb.at[0]))
        )
    ]
    for copy in halves[:1] + small + halves[1:]:
        copy.start()
    for copy in small:
        copy.wait()
    for n in range(4):
        side, kind = divmod(n, 2)
        cols = slice(n * CH, (n + 1) * CH)
        rows = pl.ds(kind * 2 * CH + side, CH, stride=2)
        wt32[rows, :] = w[:, cols].astype(F32).T
        wbt[rows, :] = jnp.broadcast_to(wb[:, cols], (CH, LANES)).T
    wt[...] = wt32[...].astype(BF16)
    gate_w_ref[...] = w[:, 4 * CH :]
    gate_b_ref[...] = jnp.broadcast_to(wb[:, 4 * CH :], gate_b_ref.shape)
    total = mask_v.shape[1]
    known = jnp.broadcast_to(mask_v[...].astype(F32), (8, total))
    index = lax.broadcasted_iota(jnp.int32, (total, LANES), 0)
    place = lax.broadcasted_iota(jnp.int32, (total, LANES), 1)
    of_axis = []
    for axis in (ROW, COL):
        chosen = index == place + lax.axis_index(axis) * SIDE
        of_axis.append(jnp.dot(known, chosen.astype(F32), preferred_element_type=F32))
    row_mask, col_mask = of_axis
    index = lax.broadcasted_iota(jnp.int32, (LANES, PIECE), 0)
    place = lax.broadcasted_iota(jnp.int32, (LANES, PIECE), 1)
    for h in range(2):
        halves[h].wait()
        for at in range(h * HALF, (h + 1) * HALF, 8):
            values = act[at : at + 8].reshape(8 * SIDE, LANES)
            off = values - jnp.mean(values, axis=-1, keepdims=True)
            spread = jnp.mean(jnp.square(off), axis=-1, keepdims=True)
            normed = off * lax.rsqrt(spread + EPS) * gain_v[...] + bias_v[...]
            normed_ref[at : at + 8] = normed.astype(BF16).reshape(8, SIDE, LANES)
    for n, piece in enumerate(pieces(SIDE)):
        rows = cat((normed_ref[k, lo : lo + width] for k, lo, width in piece), 0)
        _, lo, width = piece[0]
        step = SIDE * width // LANES
        k_of = piece[0][0] + place // LANES + (place % LANES) // width * step
        mask = jnp.dot(row_mask, (index == k_of).astype(F32), preferred_element_type=F32)
        i_of = lo + place % width
        mask = mask * jnp.dot(col_mask, (index == i_of).astype(F32), preferred_element_type=F32)
        gate, value = (
            lax.dot_general(
                wt[at : at + 2 * CH],
                rows,
                (((1,), (1,)), ((), ())),
                preferred_element_type=F32,
            )
            + across(wbt[at : at + 2 * CH])
            for at in (0, 2 * CH)
        )
        value = mask[:1] * jax.nn.sigmoid(gate) * value
        out_ref[:, n * PIECE : (n + 1) * PIECE] = value.astype(BF16)


def gather_k(values, order, wide, thin, dst_ref):
    blocks = len(order)
    for width, perm, lanes_at, col_at in (
        (WIDE, wide, 0, 0),
        (THIN, thin, SIDE * WIDE, blocks * WIDE),
    ):
        count = LANES // width
        n = SIDE // count
        groups = blocks // count
        left = cat(
            (
                cat(
                    (
                        values[
                            order[m * count + g] * 8 : (order[m * count + g] + 1) * 8,
                            lanes_at + a * LANES : lanes_at + (a + 1) * LANES,
                        ]
                        for g in range(count)
                    ),
                    1,
                )
                for m in range(groups)
                for a in range(n)
            ),
            0,
        ).astype(BF16)
        moved = jnp.dot(left, perm[...], preferred_element_type=F32).astype(BF16)
        for m in range(groups):
            for b in range(count):
                dst_ref[
                    b * n * 8 : (b + 1) * n * 8,
                    col_at + m * LANES : col_at + (m + 1) * LANES,
                ] = moved[m * n * 8 : (m + 1) * n * 8, b * LANES : (b + 1) * LANES]


def product(ref, wide, thin, left_ref, right_ref):
    core, half = lax.axis_index("core"), CH // 2
    start = pl.multiple_of((core if HALVES[0] == 0 else 1 - core) * half, half)
    gather_k(ref[0, pl.ds(start, half), :].astype(F32), [TURN.index(z) for z in PAIRS], wide, thin, left_ref)
    gather_k(ref[1].astype(F32), range(16), wide, thin, right_ref)
    return lax.dot_general(
        left_ref[...], right_ref[...], (((0,), (0,)), ((), ())), preferred_element_type=F32
    )


def build_permutations(wide_ref, thin_ref):
    for ref, width in ((wide_ref, WIDE), (thin_ref, THIN)):
        count = LANES // width
        size = count * LANES
        lane = lax.broadcasted_iota(jnp.int32, (LANES, size), 1)
        row = lax.broadcasted_iota(jnp.int32, (LANES, 1), 0)
        for g in range(count):
            goes = (row // width * count + g) * width + row % width
            ref[g * LANES : (g + 1) * LANES] = (lane == goes).astype(F32).astype(BF16)


def beside_kernel(
    mine_ref, normed_ref, w_ref, wb_ref, gain_hbm, bias_hbm, out_w_hbm, out_b_hbm,
    part_ref, gate_ref, wide_ref, thin_ref, gain_ref, bias_ref, twice_ref, out_b_ref,
    left_ref, right_ref, gain_v, bias_v, out_b_v, sem,
):
    copies = [
        pltpu.make_async_copy(src, dst, sem.at[n])
        for n, (src, dst) in enumerate(
            (
                (gain_hbm, gain_v.at[0]),
                (bias_hbm, bias_v.at[0]),
                (out_b_hbm, out_b_v.at[0]),
                (out_w_hbm, twice_ref.at[:CH]),
                (out_w_hbm, twice_ref.at[CH:]),
            )
        )
    ]
    for copy in copies:
        copy.start()
    build_permutations(wide_ref, thin_ref)
    part_ref[...] = product(mine_ref, wide_ref, thin_ref, left_ref, right_ref)
    for n, piece in enumerate(pieces(SIDE)):
        rows = cat((normed_ref[k, lo : lo + width] for k, lo, width in piece), 0)
        lin = jnp.dot(rows, w_ref[...], preferred_element_type=F32) + wb_ref[:1]
        gate_ref[n * PIECE : (n + 1) * PIECE] = jax.nn.sigmoid(lin)
    for copy in copies:
        copy.wait()
    gain_ref[...] = jnp.broadcast_to(gain_v[...], (CH, LANES)).T
    bias_ref[...] = jnp.broadcast_to(bias_v[...], (CH, LANES)).T
    out_b_ref[...] = jnp.broadcast_to(out_b_v[...], out_b_ref.shape)


def triangle_kernel(part_ref, got_ref, wide, thin, out_ref, left_ref, right_ref, tri_ref, out):
    total = part_ref[...] + product(got_ref, wide, thin, left_ref, right_ref)
    for strip in range(6):
        tri_ref[strip] = total[:, strip * LANES : (strip + 1) * LANES]

    def residue(strip, i):
        if i < WIDE:
            return tri_ref[strip, pl.ds(i, 8, stride=WIDE), :]
        return tri_ref[strip, pl.ds(8 * WIDE + i - WIDE, 8, stride=THIN), :]

    for width, perm, lanes_at, strip_at in (
        (WIDE, wide, 0, 0),
        (THIN, thin, SIDE * WIDE, 4),
    ):
        count = LANES // width
        n = SIDE // count
        groups = 16 // count
        left = cat(
            (
                cat((residue(strip_at + m, b * n + a) for b in range(count)), 1)
                for m in range(groups)
                for a in range(n)
            ),
            0,
        ).astype(BF16)
        moved = jnp.dot(left, perm[...], preferred_element_type=F32)
        for m in range(groups):
            for a in range(n):
                rows = moved[(m * n + a) * 8 : (m * n + a + 1) * 8]
                half, lane = divmod(lanes_at + a * LANES, SHARE)
                for g in range(count):
                    to = pl.ds((m * count + g) * 16 + half, 8, stride=2)
                    out[lane // LANES, to, :] = rows[:, g * LANES : (g + 1) * LANES]
    for strip in range(SHARE // LANES):
        out_ref[:, strip * LANES : (strip + 1) * LANES] = out[strip].astype(BF16)


def finish_kernel(tri_ref, gate_ref, gain_ref, bias_ref, twice_ref, wb_ref, out_hbm, out, sem):
    copies = []
    for n, piece in enumerate(pieces(SIDE)):
        half, lane = divmod(n * PIECE, SHARE)
        tri = tri_ref[half, :, lane : lane + PIECE].astype(F32)
        off = tri - jnp.mean(tri, axis=0, keepdims=True)
        spread = jnp.mean(jnp.square(off), axis=0, keepdims=True)
        mixed = off * lax.rsqrt(spread + EPS) * across(gain_ref[...]) + across(bias_ref[...])
        high = mixed.astype(BF16)
        low = (mixed - high.astype(F32)).astype(BF16)
        lin = lax.dot_general(
            cat((high, low), 0),
            twice_ref[...],
            (((0,), (0,)), ((), ())),
            preferred_element_type=F32,
        )
        update = gate_ref[n * PIECE : (n + 1) * PIECE] * (lin + wb_ref[:1])
        for at, (i, lo, width) in enumerate(piece):
            out[i, lo : lo + width] = update[at * width : (at + 1) * width]
        count = len(piece) // 3
        for i, lo, width in piece[:count]:
            where = (slice(i, i + 3), slice(lo, lo + width))
            copy = pltpu.make_async_copy(out.at[where], out_hbm.at[where], sem.at[len(copies)])
            copy.start()
            copies.append(copy)
    for copy in copies:
        copy.wait()


def call(kernel, outs, scratch=(), cost=10**9, **options):
    return pl.pallas_call(
        kernel,
        out_shape=outs,
        scratch_shapes=scratch,
        compiler_params=pltpu.CompilerParams(vmem_limit_bytes=40 * 2**20),
        cost_estimate=pl.CostEstimate(flops=cost, bytes_accessed=3 * 10**6, transcendentals=0),
        **options,
    )


def groups():
    chips = [
        [(pair * 2 + core) * 16 + z * 2 + y_hi for core in range(2)]
        for y_hi in HALVES
        for z in TURN
        for pair in PAIRS
    ]
    return [[chip[core] for chip in chips] for core in range(2)]


def stay(arrays):
    return [pltpu.with_memory_space_constraint(x, pltpu.HBM) for x in arrays]


def body(
    pair_act,
    residue_mask,
    norm_in_gain,
    norm_in_bias,
    proj_in,
    proj_bias,
    norm_out_gain,
    norm_out_bias,
    proj_out,
    out_bias,
):
    shape = jax.ShapeDtypeStruct
    vmem = pltpu.VMEM
    total = residue_mask.shape[0]
    hbm, here = pl.BlockSpec(memory_space=pltpu.HBM), pl.BlockSpec(memory_space=vmem)
    sides, normed, gate_w, gate_b = call(
        sides_kernel,
        (
            shape((2 * CH, BLOCK), BF16),
            shape((SIDE, SIDE, CH), BF16),
            shape((CH, CH), BF16),
            shape((8, CH), F32),
        ),
        [
            vmem((SIDE, SIDE, CH), F32),
            vmem((1, total), jnp.int32),
            vmem((1, CH), F32),
            vmem((1, CH), F32),
            vmem((CH, 5 * CH), BF16),
            vmem((1, 5 * CH), F32),
            vmem((4 * CH, CH), F32),
            vmem((4 * CH, CH), BF16),
            vmem((4 * CH, LANES), F32),
            pltpu.SemaphoreType.DMA((7,)),
        ],
        in_specs=[hbm] * 6,
    )(*stay((pair_act, residue_mask, norm_in_gain, norm_in_bias, proj_in, proj_bias)))
    packed = sides.reshape(CH, 2, BLOCK)
    packed = lax.all_to_all(packed, ALL, 0, 0, axis_index_groups=groups(), tiled=True)
    mine = packed.transpose(1, 0, 2)
    got = lax.ppermute(mine, "core", SWAP)
    operands = [vmem((8 * SIDE, 8 * SIDE), BF16), vmem((8 * SIDE, 16 * SIDE), BF16)]
    part, gate, wide, thin, *last = call(
        beside_kernel,
        (
            shape((8 * SIDE, 16 * SIDE), F32),
            shape((BLOCK, CH), F32),
            shape((512, 512), BF16),
            shape((1024, 1024), BF16),
            shape((CH, LANES), F32),
            shape((CH, LANES), F32),
            shape((2 * CH, CH), BF16),
            shape((8, CH), F32),
        ),
        [*operands, *[vmem((1, CH), F32)] * 3, pltpu.SemaphoreType.DMA((5,))],
        in_specs=[here] * 4 + [hbm] * 4,
    )(mine, normed, gate_w, gate_b, *stay((norm_out_gain, norm_out_bias, proj_out, out_bias)))
    triangle = call(
        triangle_kernel,
        shape((2 * CH, SHARE), BF16),
        [*operands, vmem((6, 8 * SIDE, LANES), F32), vmem((SHARE // LANES, 2 * CH, LANES), F32)],
    )(part, got, wide, thin)
    triangle = triangle.reshape(CH, 2, SHARE)
    triangle = lax.all_to_all(
        triangle, ALL, 0, 0, axis_index_groups=groups(), tiled=True
    )
    return call(
        finish_kernel,
        shape((SIDE, SIDE, CH), F32),
        [vmem((SIDE, SIDE, CH), F32), pltpu.SemaphoreType.DMA((32,))],
        out_specs=hbm,
    )(triangle.transpose(1, 0, 2), gate, *last)


def solution(mesh):
    fine = Mesh(mesh.devices.reshape(2, 4, 2, 8, 2), ROW + COL)
    return jax.shard_map(
        body,
        mesh=fine,
        in_specs=(P(ROW, COL, None), P(), P(), P(), P(), P(), P(), P(), P(), P()),
        out_specs=P(ROW, COL, None),
        check_vma=False,
    )
```

```python
import jax
import jax.numpy as jnp
from jax import lax
from jax.experimental import pallas as pl
from jax.experimental.pallas import tpu as pltpu
from jax.sharding import Mesh
from jax.sharding import PartitionSpec as P

CH = 128
ROW = ("y_lo", "x", "core")
COL = ("z", "y_hi")
ALL = ROW + COL
TURN = (6, 3, 1, 0, 7, 2, 5, 4)
PAIRS = (3, 1, 5, 4, 0, 6, 7, 2)
HALVES = (1, 0)
SWAP = [(0, 1), (1, 0)]
LANES = 128
SIDE = 48
HALF = SIDE // 2
WIDE = 32
THIN = 16
BLOCK = SIDE * SIDE
SHARE = BLOCK // 2
PIECE = 3 * LANES
F32 = jnp.float32
BF16 = jnp.bfloat16
EPS = 1e-05


def cat(parts, axis):
    return jnp.concatenate(list(parts), axis=axis)


def across(column):
    return cat([column] * (PIECE // LANES), 1)


def pieces(residues):
    for width, lo in ((WIDE, 0), (THIN, WIDE)):
        count = LANES // width
        n = residues // count
        for v in range(0, n, 3):
            yield [(b * n + u, lo, width) for u in range(v, v + 3) for b in range(count)]


def sides_kernel(
    act_hbm, mask_hbm, gain_hbm, bias_hbm, w_hbm, wb_hbm,
    out_ref, normed_ref, gate_w_ref, gate_b_ref,
    act, mask_v, gain_v, bias_v, w, wb, wt32, wt, wbt, sem,
):
    halves = [
        pltpu.make_async_copy(
            act_hbm.at[h * HALF : (h + 1) * HALF], act.at[h * HALF : (h + 1) * HALF], sem.at[h]
        )
        for h in range(2)
    ]
    small = [
        pltpu.make_async_copy(src, dst, sem.at[2 + n])
        for n, (src, dst) in enumerate(
            (
                (mask_hbm, mask_v.at[0]),
                (gain_hbm, gain_v.at[0]),
                (bias_hbm, bias_v.at[0]),
                (w_hbm, w),
                (wb_hbm, wb.at[0]),
            )
        )
    ]
    for copy in halves[:1] + small + halves[1:]:
        copy.start()
    total = mask_v.shape[1]
    index = lax.broadcasted_iota(jnp.int32, (total, LANES), 0)
    place = lax.broadcasted_iota(jnp.int32, (total, LANES), 1)
    chosen = [(index == place + lax.axis_index(axis) * SIDE).astype(F32) for axis in (ROW, COL)]
    for copy in small:
        copy.wait()
    known = jnp.broadcast_to(mask_v[...].astype(F32), (8, total))
    row_mask, col_mask = (
        jnp.dot(known, one, preferred_element_type=F32)[:, :SIDE] for one in chosen
    )
    for n in range(4):
        side, kind = divmod(n, 2)
        cols = slice(n * CH, (n + 1) * CH)
        rows = pl.ds(kind * 2 * CH + side, CH, stride=2)
        wt32[rows, :] = w[:, cols].astype(F32).T
        wbt[rows, :] = jnp.broadcast_to(wb[:, cols], (CH, LANES)).T
    wt[...] = wt32[...].astype(BF16)
    gate_w_ref[...] = w[:, 4 * CH :]
    gate_b_ref[...] = jnp.broadcast_to(wb[:, 4 * CH :], gate_b_ref.shape)
    index = lax.broadcasted_iota(jnp.int32, (SIDE, PIECE), 0)
    place = lax.broadcasted_iota(jnp.int32, (SIDE, PIECE), 1)
    for h in range(2):
        halves[h].wait()
        for at in range(h * HALF, (h + 1) * HALF, 8):
            values = act[at : at + 8].reshape(8 * SIDE, LANES)
            off = values - jnp.mean(values, axis=-1, keepdims=True)
            spread = jnp.mean(jnp.square(off), axis=-1, keepdims=True)
            normed = off * lax.rsqrt(spread + EPS) * gain_v[...] + bias_v[...]
            normed_ref[at : at + 8] = normed.astype(BF16).reshape(8, SIDE, LANES)
    for n, piece in enumerate(pieces(SIDE)):
        rows = cat((normed_ref[k, lo : lo + width] for k, lo, width in piece), 0)
        _, lo, width = piece[0]
        step = SIDE * width // LANES
        k_of = piece[0][0] + place // LANES + (place % LANES) // width * step
        mask = jnp.dot(row_mask, (index == k_of).astype(F32), preferred_element_type=F32)
        i_of = lo + place % width
        mask = mask * jnp.dot(col_mask, (index == i_of).astype(F32), preferred_element_type=F32)
        gate, value = (
            lax.dot_general(
                wt[at : at + 2 * CH],
                rows,
                (((1,), (1,)), ((), ())),
                preferred_element_type=F32,
            )
            + across(wbt[at : at + 2 * CH])
            for at in (0, 2 * CH)
        )
        value = mask[:1] * jax.nn.sigmoid(gate) * value
        out_ref[:, n * PIECE : (n + 1) * PIECE] = value.astype(BF16)


def gather_k(values, order, wide, thin, dst_ref):
    blocks = len(order)
    for width, perm, lanes_at, col_at in (
        (WIDE, wide, 0, 0),
        (THIN, thin, SIDE * WIDE, blocks * WIDE),
    ):
        count = LANES // width
        n = SIDE // count
        groups = blocks // count
        left = cat(
            (
                cat(
                    (
                        values[
                            order[m * count + g] * 8 : (order[m * count + g] + 1) * 8,
                            lanes_at + a * LANES : lanes_at + (a + 1) * LANES,
                        ]
                        for g in range(count)
                    ),
                    1,
                )
                for m in range(groups)
                for a in range(n)
            ),
            0,
        ).astype(BF16)
        moved = jnp.dot(left, perm[...], preferred_element_type=F32).astype(BF16)
        for m in range(groups):
            for b in range(count):
                dst_ref[
                    b * n * 8 : (b + 1) * n * 8,
                    col_at + m * LANES : col_at + (m + 1) * LANES,
                ] = moved[m * n * 8 : (m + 1) * n * 8, b * LANES : (b + 1) * LANES]


def product(ref, wide, thin, left_ref, right_ref):
    core, half = lax.axis_index("core"), CH // 2
    start = pl.multiple_of((core if HALVES[0] == 0 else 1 - core) * half, half)
    order = [TURN.index(z) for z in PAIRS]
    gather_k(ref[0, pl.ds(start, half), :].astype(F32), order, wide, thin, left_ref)
    gather_k(ref[1].astype(F32), range(16), wide, thin, right_ref)
    return lax.dot_general(
        left_ref[...], right_ref[...], (((0,), (0,)), ((), ())), preferred_element_type=F32
    )


def build_permutations(wide_ref, thin_ref):
    for ref, width in ((wide_ref, WIDE), (thin_ref, THIN)):
        count = LANES // width
        size = count * LANES
        lane = lax.broadcasted_iota(jnp.int32, (LANES, size), 1)
        row = lax.broadcasted_iota(jnp.int32, (LANES, 1), 0)
        for g in range(count):
            goes = (row // width * count + g) * width + row % width
            ref[g * LANES : (g + 1) * LANES] = (lane == goes).astype(F32).astype(BF16)


def beside_kernel(
    mine_ref, normed_ref, w_ref, wb_ref, gain_hbm, bias_hbm, out_w_hbm, out_b_hbm,
    part_ref, gate_ref, wide_ref, thin_ref, gain_ref, bias_ref, twice_ref, out_b_ref,
    left_ref, right_ref, gain_v, bias_v, out_b_v, sem,
):
    copies = [
        pltpu.make_async_copy(src, dst, sem.at[n])
        for n, (src, dst) in enumerate(
            (
                (gain_hbm, gain_v.at[0]),
                (bias_hbm, bias_v.at[0]),
                (out_b_hbm, out_b_v.at[0]),
                (out_w_hbm, twice_ref.at[:CH]),
                (out_w_hbm, twice_ref.at[CH:]),
            )
        )
    ]
    for copy in copies:
        copy.start()
    build_permutations(wide_ref, thin_ref)
    part_ref[...] = product(mine_ref, wide_ref, thin_ref, left_ref, right_ref)
    for n, piece in enumerate(pieces(SIDE)):
        rows = cat((normed_ref[k, lo : lo + width] for k, lo, width in piece), 0)
        lin = jnp.dot(rows, w_ref[...], preferred_element_type=F32) + wb_ref[:1]
        gate_ref[n * PIECE : (n + 1) * PIECE] = jax.nn.sigmoid(lin)
    for copy in copies:
        copy.wait()
    gain_ref[...] = jnp.broadcast_to(gain_v[...], (CH, LANES)).T
    bias_ref[...] = jnp.broadcast_to(bias_v[...], (CH, LANES)).T
    out_b_ref[...] = jnp.broadcast_to(out_b_v[...], out_b_ref.shape)


def triangle_kernel(part_ref, got_ref, wide, thin, out_ref, left_ref, right_ref, tri_ref, out):
    total = part_ref[...] + product(got_ref, wide, thin, left_ref, right_ref)
    for strip in range(6):
        tri_ref[strip] = total[:, strip * LANES : (strip + 1) * LANES]

    def residue(strip, i):
        if i < WIDE:
            return tri_ref[strip, pl.ds(i, 8, stride=WIDE), :]
        return tri_ref[strip, pl.ds(8 * WIDE + i - WIDE, 8, stride=THIN), :]

    for width, perm, lanes_at, strip_at in (
        (WIDE, wide, 0, 0),
        (THIN, thin, SIDE * WIDE, 4),
    ):
        count = LANES // width
        n = SIDE // count
        groups = 16 // count
        left = cat(
            (
                cat((residue(strip_at + m, b * n + a) for b in range(count)), 1)
                for m in range(groups)
                for a in range(n)
            ),
            0,
        ).astype(BF16)
        moved = jnp.dot(left, perm[...], preferred_element_type=F32)
        for m in range(groups):
            for a in range(n):
                rows = moved[(m * n + a) * 8 : (m * n + a + 1) * 8]
                half, lane = divmod(lanes_at + a * LANES, SHARE)
                for g in range(count):
                    to = pl.ds((m * count + g) * 16 + half, 8, stride=2)
                    out[lane // LANES, to, :] = rows[:, g * LANES : (g + 1) * LANES]
    for strip in range(SHARE // LANES):
        out_ref[:, strip * LANES : (strip + 1) * LANES] = out[strip].astype(BF16)


def finish_kernel(tri_ref, gate_ref, gain_ref, bias_ref, twice_ref, wb_ref, out_hbm, out, sem):
    copies = []
    for n, piece in enumerate(pieces(SIDE)):
        half, lane = divmod(n * PIECE, SHARE)
        tri = tri_ref[half, :, lane : lane + PIECE].astype(F32)
        off = tri - jnp.mean(tri, axis=0, keepdims=True)
        spread = jnp.mean(jnp.square(off), axis=0, keepdims=True)
        mixed = off * lax.rsqrt(spread + EPS) * across(gain_ref[...]) + across(bias_ref[...])
        high = mixed.astype(BF16)
        low = (mixed - high.astype(F32)).astype(BF16)
        lin = lax.dot_general(
            cat((high, low), 0),
            twice_ref[...],
            (((0,), (0,)), ((), ())),
            preferred_element_type=F32,
        )
        update = gate_ref[n * PIECE : (n + 1) * PIECE] * (lin + wb_ref[:1])
        for at, (i, lo, width) in enumerate(piece):
            out[i, lo : lo + width] = update[at * width : (at + 1) * width]
        count = len(piece) // 3
        for i, lo, width in piece[:count]:
            where = (slice(i, i + 3), slice(lo, lo + width))
            copy = pltpu.make_async_copy(out.at[where], out_hbm.at[where], sem.at[len(copies)])
            copy.start()
            copies.append(copy)
    for copy in copies:
        copy.wait()


def call(kernel, outs, scratch=(), cost=10**9, **options):
    return pl.pallas_call(
        kernel,
        out_shape=outs,
        scratch_shapes=scratch,
        compiler_params=pltpu.CompilerParams(vmem_limit_bytes=40 * 2**20),
        cost_estimate=pl.CostEstimate(flops=cost, bytes_accessed=3 * 10**6, transcendentals=0),
        **options,
    )


def groups():
    chips = [
        [(pair * 2 + core) * 16 + z * 2 + y_hi for core in range(2)]
        for y_hi in HALVES
        for z in TURN
        for pair in PAIRS
    ]
    return [[chip[core] for chip in chips] for core in range(2)]


def stay(arrays):
    return [pltpu.with_memory_space_constraint(x, pltpu.HBM) for x in arrays]


def body(
    pair_act,
    residue_mask,
    norm_in_gain,
    norm_in_bias,
    proj_in,
    proj_bias,
    norm_out_gain,
    norm_out_bias,
    proj_out,
    out_bias,
):
    shape = jax.ShapeDtypeStruct
    vmem = pltpu.VMEM
    total = residue_mask.shape[0]
    hbm, here = pl.BlockSpec(memory_space=pltpu.HBM), pl.BlockSpec(memory_space=vmem)
    sides, normed, gate_w, gate_b = call(
        sides_kernel,
        (
            shape((2 * CH, BLOCK), BF16),
            shape((SIDE, SIDE, CH), BF16),
            shape((CH, CH), BF16),
            shape((8, CH), F32),
        ),
        [
            vmem((SIDE, SIDE, CH), F32),
            vmem((1, total), jnp.int32),
            vmem((1, CH), F32),
            vmem((1, CH), F32),
            vmem((CH, 5 * CH), BF16),
            vmem((1, 5 * CH), F32),
            vmem((4 * CH, CH), F32),
            vmem((4 * CH, CH), BF16),
            vmem((4 * CH, LANES), F32),
            pltpu.SemaphoreType.DMA((7,)),
        ],
        in_specs=[hbm] * 6,
    )(*stay((pair_act, residue_mask, norm_in_gain, norm_in_bias, proj_in, proj_bias)))
    packed = sides.reshape(CH, 2, BLOCK)
    packed = lax.all_to_all(packed, ALL, 0, 0, axis_index_groups=groups(), tiled=True)
    mine = packed.transpose(1, 0, 2)
    got = lax.ppermute(mine, "core", SWAP)
    operands = [vmem((8 * SIDE, 8 * SIDE), BF16), vmem((8 * SIDE, 16 * SIDE), BF16)]
    part, gate, wide, thin, *last = call(
        beside_kernel,
        (
            shape((8 * SIDE, 16 * SIDE), F32),
            shape((BLOCK, CH), F32),
            shape((512, 512), BF16),
            shape((1024, 1024), BF16),
            shape((CH, LANES), F32),
            shape((CH, LANES), F32),
            shape((2 * CH, CH), BF16),
            shape((8, CH), F32),
        ),
        [*operands, *[vmem((1, CH), F32)] * 3, pltpu.SemaphoreType.DMA((5,))],
        in_specs=[here] * 4 + [hbm] * 4,
    )(mine, normed, gate_w, gate_b, *stay((norm_out_gain, norm_out_bias, proj_out, out_bias)))
    triangle = call(
        triangle_kernel,
        shape((2 * CH, SHARE), BF16),
        [*operands, vmem((6, 8 * SIDE, LANES), F32), vmem((SHARE // LANES, 2 * CH, LANES), F32)],
    )(part, got, wide, thin)
    triangle = triangle.reshape(CH, 2, SHARE)
    triangle = lax.all_to_all(
        triangle, ALL, 0, 0, axis_index_groups=groups(), tiled=True
    )
    return call(
        finish_kernel,
        shape((SIDE, SIDE, CH), F32),
        [vmem((SIDE, SIDE, CH), F32), pltpu.SemaphoreType.DMA((32,))],
        out_specs=hbm,
    )(triangle.transpose(1, 0, 2), gate, *last)


def solution(mesh):
    fine = Mesh(mesh.devices.reshape(2, 4, 2, 8, 2), ROW + COL)
    return jax.shard_map(
        body,
        mesh=fine,
        in_specs=(P(ROW, COL, None), P(), P(), P(), P(), P(), P(), P(), P(), P()),
        out_specs=P(ROW, COL, None),
        check_vma=False,
    )
```

```python
import jax
import jax.numpy as jnp
from jax import lax
from jax.experimental import pallas as pl
from jax.experimental.pallas import tpu as pltpu
from jax.sharding import Mesh
from jax.sharding import PartitionSpec as P

CH = 128
ROW = ("y_lo", "x", "core")
COL = ("z", "y_hi")
ALL = ROW + COL
TURN = (6, 3, 1, 0, 7, 2, 5, 4)
PAIRS = (3, 1, 5, 4, 0, 6, 7, 2)
HALVES = (1, 0)
SWAP = [(0, 1), (1, 0)]
LANES = 128
SIDE = 48
HALF = SIDE // 2
WIDE = 32
THIN = 16
BLOCK = SIDE * SIDE
SHARE = BLOCK // 2
PIECE = 3 * LANES
F32 = jnp.float32
BF16 = jnp.bfloat16
EPS = 1e-05


def cat(parts, axis):
    return jnp.concatenate(list(parts), axis=axis)


def across(column):
    return cat([column] * (PIECE // LANES), 1)


def pieces(residues):
    for width, lo in ((WIDE, 0), (THIN, WIDE)):
        count = LANES // width
        n = residues // count
        for v in range(0, n, 3):
            yield [(b * n + u, lo, width) for u in range(v, v + 3) for b in range(count)]


def sides_kernel(
    act_hbm, mask_hbm, gain_hbm, bias_hbm, w_hbm, wb_hbm,
    out_ref, normed_ref, gate_w_ref, gate_b_ref,
    act, mask_v, gain_v, bias_v, w, wb, wt32, wt, wbt, sem,
):
    halves = [
        pltpu.make_async_copy(
            act_hbm.at[h * HALF : (h + 1) * HALF], act.at[h * HALF : (h + 1) * HALF], sem.at[h]
        )
        for h in range(2)
    ]
    small = [
        pltpu.make_async_copy(src, dst, sem.at[2 + n])
        for n, (src, dst) in enumerate(
            (
                (mask_hbm, mask_v.at[0]),
                (gain_hbm, gain_v.at[0]),
                (bias_hbm, bias_v.at[0]),
                (w_hbm, w),
                (wb_hbm, wb.at[0]),
            )
        )
    ]
    for copy in halves[:1] + small + halves[1:]:
        copy.start()
    total = mask_v.shape[1]
    index = lax.broadcasted_iota(jnp.int32, (total, LANES), 0)
    place = lax.broadcasted_iota(jnp.int32, (total, LANES), 1)
    chosen = [(index == place + lax.axis_index(axis) * SIDE).astype(F32) for axis in (ROW, COL)]
    for copy in small:
        copy.wait()
    known = jnp.broadcast_to(mask_v[...].astype(F32), (8, total))
    row_mask, col_mask = (
        jnp.dot(known, one, preferred_element_type=F32)[:, :SIDE] for one in chosen
    )
    for n in range(4):
        side, kind = divmod(n, 2)
        cols = slice(n * CH, (n + 1) * CH)
        rows = pl.ds(kind * 2 * CH + side, CH, stride=2)
        wt32[rows, :] = w[:, cols].astype(F32).T
        wbt[rows, :] = jnp.broadcast_to(wb[:, cols], (CH, LANES)).T
    wt[...] = wt32[...].astype(BF16)
    gate_w_ref[...] = w[:, 4 * CH :]
    gate_b_ref[...] = jnp.broadcast_to(wb[:, 4 * CH :], gate_b_ref.shape)
    index = lax.broadcasted_iota(jnp.int32, (SIDE, PIECE), 0)
    place = lax.broadcasted_iota(jnp.int32, (SIDE, PIECE), 1)
    for h in range(2):
        halves[h].wait()
        for at in range(h * HALF, (h + 1) * HALF, 8):
            values = act[at : at + 8].reshape(8 * SIDE, LANES)
            off = values - jnp.mean(values, axis=-1, keepdims=True)
            spread = jnp.mean(jnp.square(off), axis=-1, keepdims=True)
            normed = off * lax.rsqrt(spread + EPS) * gain_v[...] + bias_v[...]
            normed_ref[at : at + 8] = normed.astype(BF16).reshape(8, SIDE, LANES)
    for n, piece in enumerate(pieces(SIDE)):
        rows = cat((normed_ref[k, lo : lo + width] for k, lo, width in piece), 0)
        _, lo, width = piece[0]
        step = SIDE * width // LANES
        k_of = piece[0][0] + place // LANES + (place % LANES) // width * step
        mask = jnp.dot(row_mask, (index == k_of).astype(F32), preferred_element_type=F32)
        i_of = lo + place % width
        mask = mask * jnp.dot(col_mask, (index == i_of).astype(F32), preferred_element_type=F32)
        gate, value = (
            lax.dot_general(
                wt[at : at + 2 * CH],
                rows,
                (((1,), (1,)), ((), ())),
                preferred_element_type=F32,
            )
            + across(wbt[at : at + 2 * CH])
            for at in (0, 2 * CH)
        )
        value = mask[:1] * jax.nn.sigmoid(gate) * value
        out_ref[:, n * PIECE : (n + 1) * PIECE] = value.astype(BF16)


def gather_k(values, order, wide, thin, dst_ref):
    blocks = len(order)
    for width, perm, lanes_at, col_at in (
        (WIDE, wide, 0, 0),
        (THIN, thin, SIDE * WIDE, blocks * WIDE),
    ):
        count = LANES // width
        n = SIDE // count
        groups = blocks // count
        left = cat(
            (
                cat(
                    (
                        values[
                            order[m * count + g] * 8 : (order[m * count + g] + 1) * 8,
                            lanes_at + a * LANES : lanes_at + (a + 1) * LANES,
                        ]
                        for g in range(count)
                    ),
                    1,
                )
                for m in range(groups)
                for a in range(n)
            ),
            0,
        ).astype(BF16)
        moved = jnp.dot(left, perm[...], preferred_element_type=F32).astype(BF16)
        for m in range(groups):
            for b in range(count):
                dst_ref[
                    b * n * 8 : (b + 1) * n * 8,
                    col_at + m * LANES : col_at + (m + 1) * LANES,
                ] = moved[m * n * 8 : (m + 1) * n * 8, b * LANES : (b + 1) * LANES]


def product(ref, wide, thin, left_ref, right_ref):
    core, half = lax.axis_index("core"), CH // 2
    start = pl.multiple_of((core if HALVES[0] == 0 else 1 - core) * half, half)
    order = [TURN.index(z) for z in PAIRS]
    gather_k(ref[0, pl.ds(start, half), :].astype(F32), order, wide, thin, left_ref)
    gather_k(ref[1].astype(F32), range(16), wide, thin, right_ref)
    return lax.dot_general(
        left_ref[...], right_ref[...], (((0,), (0,)), ((), ())), preferred_element_type=F32
    )


def build_permutations(wide_ref, thin_ref):
    for ref, width in ((wide_ref, WIDE), (thin_ref, THIN)):
        count = LANES // width
        ref[...] = jnp.zeros(ref.shape, BF16)
        lane = lax.broadcasted_iota(jnp.int32, (width, LANES), 1)
        row = lax.broadcasted_iota(jnp.int32, (width, LANES), 0)
        for g in range(count):
            one = (lane == g * width + row).astype(F32).astype(BF16)
            for b in range(count):
                at = g * LANES + b * width
                ref[at : at + width, b * LANES : (b + 1) * LANES] = one


def beside_kernel(
    mine_ref, normed_ref, w_ref, wb_ref, gain_hbm, bias_hbm, out_w_hbm, out_b_hbm,
    part_ref, gate_ref, wide_ref, thin_ref, gain_ref, bias_ref, twice_ref, out_b_ref,
    left_ref, right_ref, gain_v, bias_v, out_b_v, sem,
):
    copies = [
        pltpu.make_async_copy(src, dst, sem.at[n])
        for n, (src, dst) in enumerate(
            (
                (gain_hbm, gain_v.at[0]),
                (bias_hbm, bias_v.at[0]),
                (out_b_hbm, out_b_v.at[0]),
                (out_w_hbm, twice_ref.at[:CH]),
                (out_w_hbm, twice_ref.at[CH:]),
            )
        )
    ]
    for copy in copies:
        copy.start()
    build_permutations(wide_ref, thin_ref)
    part_ref[...] = product(mine_ref, wide_ref, thin_ref, left_ref, right_ref)
    for n, piece in enumerate(pieces(SIDE)):
        rows = cat((normed_ref[k, lo : lo + width] for k, lo, width in piece), 0)
        lin = jnp.dot(rows, w_ref[...], preferred_element_type=F32) + wb_ref[:1]
        gate_ref[n * PIECE : (n + 1) * PIECE] = jax.nn.sigmoid(lin)
    for copy in copies:
        copy.wait()
    gain_ref[...] = jnp.broadcast_to(gain_v[...], (CH, LANES)).T
    bias_ref[...] = jnp.broadcast_to(bias_v[...], (CH, LANES)).T
    out_b_ref[...] = jnp.broadcast_to(out_b_v[...], out_b_ref.shape)


def triangle_kernel(part_ref, got_ref, wide, thin, out_ref, left_ref, right_ref, tri_ref, out):
    total = part_ref[...] + product(got_ref, wide, thin, left_ref, right_ref)
    for strip in range(6):
        tri_ref[strip] = total[:, strip * LANES : (strip + 1) * LANES]

    def residue(strip, i):
        if i < WIDE:
            return tri_ref[strip, pl.ds(i, 8, stride=WIDE), :]
        return tri_ref[strip, pl.ds(8 * WIDE + i - WIDE, 8, stride=THIN), :]

    for width, perm, lanes_at, strip_at in (
        (WIDE, wide, 0, 0),
        (THIN, thin, SIDE * WIDE, 4),
    ):
        count = LANES // width
        n = SIDE // count
        groups = 16 // count
        left = cat(
            (
                cat((residue(strip_at + m, b * n + a) for b in range(count)), 1)
                for m in range(groups)
                for a in range(n)
            ),
            0,
        ).astype(BF16)
        moved = jnp.dot(left, perm[...], preferred_element_type=F32)
        for m in range(groups):
            for a in range(n):
                rows = moved[(m * n + a) * 8 : (m * n + a + 1) * 8]
                half, lane = divmod(lanes_at + a * LANES, SHARE)
                for g in range(count):
                    to = pl.ds((m * count + g) * 16 + half, 8, stride=2)
                    out[lane // LANES, to, :] = rows[:, g * LANES : (g + 1) * LANES]
    for strip in range(SHARE // LANES):
        out_ref[:, strip * LANES : (strip + 1) * LANES] = out[strip].astype(BF16)


def finish_kernel(tri_ref, gate_ref, gain_ref, bias_ref, twice_ref, wb_ref, out_hbm, out, sem):
    copies = []
    for n, piece in enumerate(pieces(SIDE)):
        half, lane = divmod(n * PIECE, SHARE)
        tri = tri_ref[half, :, lane : lane + PIECE].astype(F32)
        off = tri - jnp.mean(tri, axis=0, keepdims=True)
        spread = jnp.mean(jnp.square(off), axis=0, keepdims=True)
        mixed = off * lax.rsqrt(spread + EPS) * across(gain_ref[...]) + across(bias_ref[...])
        high = mixed.astype(BF16)
        low = (mixed - high.astype(F32)).astype(BF16)
        lin = lax.dot_general(
            cat((high, low), 0),
            twice_ref[...],
            (((0,), (0,)), ((), ())),
            preferred_element_type=F32,
        )
        update = gate_ref[n * PIECE : (n + 1) * PIECE] * (lin + wb_ref[:1])
        for at, (i, lo, width) in enumerate(piece):
            out[i, lo : lo + width] = update[at * width : (at + 1) * width]
        count = len(piece) // 3
        for i, lo, width in piece[:count]:
            where = (slice(i, i + 3), slice(lo, lo + width))
            copy = pltpu.make_async_copy(out.at[where], out_hbm.at[where], sem.at[len(copies)])
            copy.start()
            copies.append(copy)
    for copy in copies:
        copy.wait()


def call(kernel, outs, scratch=(), cost=10**9, **options):
    return pl.pallas_call(
        kernel,
        out_shape=outs,
        scratch_shapes=scratch,
        compiler_params=pltpu.CompilerParams(vmem_limit_bytes=40 * 2**20),
        cost_estimate=pl.CostEstimate(flops=cost, bytes_accessed=3 * 10**6, transcendentals=0),
        **options,
    )


def groups():
    chips = [
        [(pair * 2 + core) * 16 + z * 2 + y_hi for core in range(2)]
        for y_hi in HALVES
        for z in TURN
        for pair in PAIRS
    ]
    return [[chip[core] for chip in chips] for core in range(2)]


def stay(arrays):
    return [pltpu.with_memory_space_constraint(x, pltpu.HBM) for x in arrays]


def body(
    pair_act,
    residue_mask,
    norm_in_gain,
    norm_in_bias,
    proj_in,
    proj_bias,
    norm_out_gain,
    norm_out_bias,
    proj_out,
    out_bias,
):
    shape = jax.ShapeDtypeStruct
    vmem = pltpu.VMEM
    total = residue_mask.shape[0]
    hbm, here = pl.BlockSpec(memory_space=pltpu.HBM), pl.BlockSpec(memory_space=vmem)
    sides, normed, gate_w, gate_b = call(
        sides_kernel,
        (
            shape((2 * CH, BLOCK), BF16),
            shape((SIDE, SIDE, CH), BF16),
            shape((CH, CH), BF16),
            shape((8, CH), F32),
        ),
        [
            vmem((SIDE, SIDE, CH), F32),
            vmem((1, total), jnp.int32),
            vmem((1, CH), F32),
            vmem((1, CH), F32),
            vmem((CH, 5 * CH), BF16),
            vmem((1, 5 * CH), F32),
            vmem((4 * CH, CH), F32),
            vmem((4 * CH, CH), BF16),
            vmem((4 * CH, LANES), F32),
            pltpu.SemaphoreType.DMA((7,)),
        ],
        in_specs=[hbm] * 6,
    )(*stay((pair_act, residue_mask, norm_in_gain, norm_in_bias, proj_in, proj_bias)))
    packed = sides.reshape(CH, 2, BLOCK)
    packed = lax.all_to_all(packed, ALL, 0, 0, axis_index_groups=groups(), tiled=True)
    mine = packed.transpose(1, 0, 2)
    got = lax.ppermute(mine, "core", SWAP)
    operands = [vmem((8 * SIDE, 8 * SIDE), BF16), vmem((8 * SIDE, 16 * SIDE), BF16)]
    part, gate, wide, thin, *last = call(
        beside_kernel,
        (
            shape((8 * SIDE, 16 * SIDE), F32),
            shape((BLOCK, CH), F32),
            shape((512, 512), BF16),
            shape((1024, 1024), BF16),
            shape((CH, LANES), F32),
            shape((CH, LANES), F32),
            shape((2 * CH, CH), BF16),
            shape((8, CH), F32),
        ),
        [*operands, *[vmem((1, CH), F32)] * 3, pltpu.SemaphoreType.DMA((5,))],
        in_specs=[here] * 4 + [hbm] * 4,
    )(mine, normed, gate_w, gate_b, *stay((norm_out_gain, norm_out_bias, proj_out, out_bias)))
    triangle = call(
        triangle_kernel,
        shape((2 * CH, SHARE), BF16),
        [*operands, vmem((6, 8 * SIDE, LANES), F32), vmem((SHARE // LANES, 2 * CH, LANES), F32)],
    )(part, got, wide, thin)
    triangle = triangle.reshape(CH, 2, SHARE)
    triangle = lax.all_to_all(
        triangle, ALL, 0, 0, axis_index_groups=groups(), tiled=True
    )
    return call(
        finish_kernel,
        shape((SIDE, SIDE, CH), F32),
        [vmem((SIDE, SIDE, CH), F32), pltpu.SemaphoreType.DMA((32,))],
        out_specs=hbm,
    )(triangle.transpose(1, 0, 2), gate, *last)


def solution(mesh):
    fine = Mesh(mesh.devices.reshape(2, 4, 2, 8, 2), ROW + COL)
    return jax.shard_map(
        body,
        mesh=fine,
        in_specs=(P(ROW, COL, None), P(), P(), P(), P(), P(), P(), P(), P(), P()),
        out_specs=P(ROW, COL, None),
        check_vma=False,
    )
```

```python
import jax
import jax.numpy as jnp
from jax import lax
from jax.experimental import pallas as pl
from jax.experimental.pallas import tpu as pltpu
from jax.sharding import Mesh
from jax.sharding import PartitionSpec as P

CH = 128
ROW = ("y_lo", "x", "core")
COL = ("z", "y_hi")
ALL = ROW + COL
TURN = (6, 3, 1, 0, 7, 2, 5, 4)
PAIRS = (3, 1, 5, 4, 0, 6, 7, 2)
HALVES = (1, 0)
SWAP = [(0, 1), (1, 0)]
LANES = 128
SIDE = 48
PARTS = 1
PART = SIDE // PARTS
WIDE = 32
THIN = 16
BLOCK = SIDE * SIDE
SHARE = BLOCK // 2
PIECE = 3 * LANES
F32 = jnp.float32
BF16 = jnp.bfloat16
EPS = 1e-05


def cat(parts, axis):
    return jnp.concatenate(list(parts), axis=axis)


def across(column):
    return cat([column] * (PIECE // LANES), 1)


def pieces(residues):
    for width, lo in ((WIDE, 0), (THIN, WIDE)):
        count = LANES // width
        n = residues // count
        for v in range(0, n, 3):
            yield [(b * n + u, lo, width) for u in range(v, v + 3) for b in range(count)]


def sides_kernel(
    act_hbm, mask_hbm, gain_hbm, bias_hbm, w_hbm, wb_hbm,
    out_ref, normed_ref, gate_w_ref, gate_b_ref,
    act, mask_v, gain_v, bias_v, w, wb, wt32, wt, wbt, sem,
):
    parts_in = [
        pltpu.make_async_copy(
            act_hbm.at[h * PART : (h + 1) * PART], act.at[h * PART : (h + 1) * PART], sem.at[h]
        )
        for h in range(PARTS)
    ]
    small = [
        pltpu.make_async_copy(src, dst, sem.at[PARTS + n])
        for n, (src, dst) in enumerate(
            (
                (mask_hbm, mask_v.at[0]),
                (gain_hbm, gain_v.at[0]),
                (bias_hbm, bias_v.at[0]),
                (w_hbm, w),
                (wb_hbm, wb.at[0]),
            )
        )
    ]
    for copy in parts_in[:1] + small + parts_in[1:]:
        copy.start()
    total = mask_v.shape[1]
    index = lax.broadcasted_iota(jnp.int32, (total, LANES), 0)
    place = lax.broadcasted_iota(jnp.int32, (total, LANES), 1)
    chosen = [(index == place + lax.axis_index(axis) * SIDE).astype(F32) for axis in (ROW, COL)]
    for copy in small:
        copy.wait()
    known = jnp.broadcast_to(mask_v[...].astype(F32), (8, total))
    row_mask, col_mask = (
        jnp.dot(known, one, preferred_element_type=F32)[:, :SIDE] for one in chosen
    )
    for n in range(4):
        side, kind = divmod(n, 2)
        cols = slice(n * CH, (n + 1) * CH)
        rows = pl.ds(kind * 2 * CH + side, CH, stride=2)
        wt32[rows, :] = w[:, cols].astype(F32).T
        wbt[rows, :] = jnp.broadcast_to(wb[:, cols], (CH, LANES)).T
    wt[...] = wt32[...].astype(BF16)
    gate_w_ref[...] = w[:, 4 * CH :]
    gate_b_ref[...] = jnp.broadcast_to(wb[:, 4 * CH :], gate_b_ref.shape)
    index = lax.broadcasted_iota(jnp.int32, (SIDE, PIECE), 0)
    place = lax.broadcasted_iota(jnp.int32, (SIDE, PIECE), 1)
    for h in range(PARTS):
        parts_in[h].wait()
        for at in range(h * PART, (h + 1) * PART, 8):
            values = act[at : at + 8].reshape(8 * SIDE, LANES)
            off = values - jnp.mean(values, axis=-1, keepdims=True)
            spread = jnp.mean(jnp.square(off), axis=-1, keepdims=True)
            normed = off * lax.rsqrt(spread + EPS) * gain_v[...] + bias_v[...]
            normed_ref[at : at + 8] = normed.astype(BF16).reshape(8, SIDE, LANES)
    for n, piece in enumerate(pieces(SIDE)):
        rows = cat((normed_ref[k, lo : lo + width] for k, lo, width in piece), 0)
        _, lo, width = piece[0]
        step = SIDE * width // LANES
        k_of = piece[0][0] + place // LANES + (place % LANES) // width * step
        mask = jnp.dot(row_mask, (index == k_of).astype(F32), preferred_element_type=F32)
        i_of = lo + place % width
        mask = mask * jnp.dot(col_mask, (index == i_of).astype(F32), preferred_element_type=F32)
        gate, value = (
            lax.dot_general(
                wt[at : at + 2 * CH],
                rows,
                (((1,), (1,)), ((), ())),
                preferred_element_type=F32,
            )
            + across(wbt[at : at + 2 * CH])
            for at in (0, 2 * CH)
        )
        value = mask[:1] * jax.nn.sigmoid(gate) * value
        out_ref[:, n * PIECE : (n + 1) * PIECE] = value.astype(BF16)


def gather_k(values, order, wide, thin, dst_ref):
    blocks = len(order)
    for width, perm, lanes_at, col_at in (
        (WIDE, wide, 0, 0),
        (THIN, thin, SIDE * WIDE, blocks * WIDE),
    ):
        count = LANES // width
        n = SIDE // count
        groups = blocks // count
        left = cat(
            (
                cat(
                    (
                        values[
                            order[m * count + g] * 8 : (order[m * count + g] + 1) * 8,
                            lanes_at + a * LANES : lanes_at + (a + 1) * LANES,
                        ]
                        for g in range(count)
                    ),
                    1,
                )
                for m in range(groups)
                for a in range(n)
            ),
            0,
        ).astype(BF16)
        moved = jnp.dot(left, perm[...], preferred_element_type=F32).astype(BF16)
        for m in range(groups):
            for b in range(count):
                dst_ref[
                    b * n * 8 : (b + 1) * n * 8,
                    col_at + m * LANES : col_at + (m + 1) * LANES,
                ] = moved[m * n * 8 : (m + 1) * n * 8, b * LANES : (b + 1) * LANES]


def product(ref, wide, thin, left_ref, right_ref):
    core, half = lax.axis_index("core"), CH // 2
    start = pl.multiple_of((core if HALVES[0] == 0 else 1 - core) * half, half)
    order = [TURN.index(z) for z in PAIRS]
    gather_k(ref[0, pl.ds(start, half), :].astype(F32), order, wide, thin, left_ref)
    gather_k(ref[1].astype(F32), range(16), wide, thin, right_ref)
    return lax.dot_general(
        left_ref[...], right_ref[...], (((0,), (0,)), ((), ())), preferred_element_type=F32
    )


def build_permutations(wide_ref, thin_ref):
    for ref, width in ((wide_ref, WIDE), (thin_ref, THIN)):
        count = LANES // width
        ref[...] = jnp.zeros(ref.shape, BF16)
        lane = lax.broadcasted_iota(jnp.int32, (width, LANES), 1)
        row = lax.broadcasted_iota(jnp.int32, (width, LANES), 0)
        for g in range(count):
            one = (lane == g * width + row).astype(F32).astype(BF16)
            for b in range(count):
                at = g * LANES + b * width
                ref[at : at + width, b * LANES : (b + 1) * LANES] = one


def beside_kernel(
    mine_ref, normed_ref, w_ref, wb_ref, gain_hbm, bias_hbm, out_w_hbm, out_b_hbm,
    part_ref, gate_ref, wide_ref, thin_ref, gain_ref, bias_ref, twice_ref, out_b_ref,
    left_ref, right_ref, gain_v, bias_v, out_b_v, sem,
):
    copies = [
        pltpu.make_async_copy(src, dst, sem.at[n])
        for n, (src, dst) in enumerate(
            (
                (gain_hbm, gain_v.at[0]),
                (bias_hbm, bias_v.at[0]),
                (out_b_hbm, out_b_v.at[0]),
                (out_w_hbm, twice_ref.at[:CH]),
                (out_w_hbm, twice_ref.at[CH:]),
            )
        )
    ]
    for copy in copies:
        copy.start()
    build_permutations(wide_ref, thin_ref)
    part_ref[...] = product(mine_ref, wide_ref, thin_ref, left_ref, right_ref)
    for n, piece in enumerate(pieces(SIDE)):
        rows = cat((normed_ref[k, lo : lo + width] for k, lo, width in piece), 0)
        lin = jnp.dot(rows, w_ref[...], preferred_element_type=F32) + wb_ref[:1]
        gate_ref[n * PIECE : (n + 1) * PIECE] = jax.nn.sigmoid(lin)
    for copy in copies:
        copy.wait()
    gain_ref[...] = jnp.broadcast_to(gain_v[...], (CH, LANES)).T
    bias_ref[...] = jnp.broadcast_to(bias_v[...], (CH, LANES)).T
    out_b_ref[...] = jnp.broadcast_to(out_b_v[...], out_b_ref.shape)


def triangle_kernel(part_ref, got_ref, wide, thin, out_ref, left_ref, right_ref, tri_ref, out):
    total = part_ref[...] + product(got_ref, wide, thin, left_ref, right_ref)
    for strip in range(6):
        tri_ref[strip] = total[:, strip * LANES : (strip + 1) * LANES]

    def residue(strip, i):
        if i < WIDE:
            return tri_ref[strip, pl.ds(i, 8, stride=WIDE), :]
        return tri_ref[strip, pl.ds(8 * WIDE + i - WIDE, 8, stride=THIN), :]

    for width, perm, lanes_at, strip_at in (
        (WIDE, wide, 0, 0),
        (THIN, thin, SIDE * WIDE, 4),
    ):
        count = LANES // width
        n = SIDE // count
        groups = 16 // count
        left = cat(
            (
                cat((residue(strip_at + m, b * n + a) for b in range(count)), 1)
                for m in range(groups)
                for a in range(n)
            ),
            0,
        ).astype(BF16)
        moved = jnp.dot(left, perm[...], preferred_element_type=F32)
        for m in range(groups):
            for a in range(n):
                rows = moved[(m * n + a) * 8 : (m * n + a + 1) * 8]
                half, lane = divmod(lanes_at + a * LANES, SHARE)
                for g in range(count):
                    to = pl.ds((m * count + g) * 16 + half, 8, stride=2)
                    out[lane // LANES, to, :] = rows[:, g * LANES : (g + 1) * LANES]
    for strip in range(SHARE // LANES):
        out_ref[:, strip * LANES : (strip + 1) * LANES] = out[strip].astype(BF16)


def finish_kernel(tri_ref, gate_ref, gain_ref, bias_ref, twice_ref, wb_ref, out_hbm, out, sem):
    copies = []
    for n, piece in enumerate(pieces(SIDE)):
        half, lane = divmod(n * PIECE, SHARE)
        tri = tri_ref[half, :, lane : lane + PIECE].astype(F32)
        off = tri - jnp.mean(tri, axis=0, keepdims=True)
        spread = jnp.mean(jnp.square(off), axis=0, keepdims=True)
        mixed = off * lax.rsqrt(spread + EPS) * across(gain_ref[...]) + across(bias_ref[...])
        high = mixed.astype(BF16)
        low = (mixed - high.astype(F32)).astype(BF16)
        lin = lax.dot_general(
            cat((high, low), 0),
            twice_ref[...],
            (((0,), (0,)), ((), ())),
            preferred_element_type=F32,
        )
        update = gate_ref[n * PIECE : (n + 1) * PIECE] * (lin + wb_ref[:1])
        for at, (i, lo, width) in enumerate(piece):
            out[i, lo : lo + width] = update[at * width : (at + 1) * width]
        count = len(piece) // 3
        for i, lo, width in piece[:count]:
            where = (slice(i, i + 3), slice(lo, lo + width))
            copy = pltpu.make_async_copy(out.at[where], out_hbm.at[where], sem.at[len(copies)])
            copy.start()
            copies.append(copy)
    for copy in copies:
        copy.wait()


def call(kernel, outs, scratch=(), cost=10**9, **options):
    return pl.pallas_call(
        kernel,
        out_shape=outs,
        scratch_shapes=scratch,
        compiler_params=pltpu.CompilerParams(vmem_limit_bytes=40 * 2**20),
        cost_estimate=pl.CostEstimate(flops=cost, bytes_accessed=3 * 10**6, transcendentals=0),
        **options,
    )


def groups():
    chips = [
        [(pair * 2 + core) * 16 + z * 2 + y_hi for core in range(2)]
        for y_hi in HALVES
        for z in TURN
        for pair in PAIRS
    ]
    return [[chip[core] for chip in chips] for core in range(2)]


def stay(arrays):
    return [pltpu.with_memory_space_constraint(x, pltpu.HBM) for x in arrays]


def body(
    pair_act,
    residue_mask,
    norm_in_gain,
    norm_in_bias,
    proj_in,
    proj_bias,
    norm_out_gain,
    norm_out_bias,
    proj_out,
    out_bias,
):
    shape = jax.ShapeDtypeStruct
    vmem = pltpu.VMEM
    total = residue_mask.shape[0]
    hbm, here = pl.BlockSpec(memory_space=pltpu.HBM), pl.BlockSpec(memory_space=vmem)
    sides, normed, gate_w, gate_b = call(
        sides_kernel,
        (
            shape((2 * CH, BLOCK), BF16),
            shape((SIDE, SIDE, CH), BF16),
            shape((CH, CH), BF16),
            shape((8, CH), F32),
        ),
        [
            vmem((SIDE, SIDE, CH), F32),
            vmem((1, total), jnp.int32),
            vmem((1, CH), F32),
            vmem((1, CH), F32),
            vmem((CH, 5 * CH), BF16),
            vmem((1, 5 * CH), F32),
            vmem((4 * CH, CH), F32),
            vmem((4 * CH, CH), BF16),
            vmem((4 * CH, LANES), F32),
            pltpu.SemaphoreType.DMA((PARTS + 5,)),
        ],
        in_specs=[hbm] * 6,
    )(*stay((pair_act, residue_mask, norm_in_gain, norm_in_bias, proj_in, proj_bias)))
    packed = sides.reshape(CH, 2, BLOCK)
    packed = lax.all_to_all(packed, ALL, 0, 0, axis_index_groups=groups(), tiled=True)
    mine = packed.transpose(1, 0, 2)
    got = lax.ppermute(mine, "core", SWAP)
    operands = [vmem((8 * SIDE, 8 * SIDE), BF16), vmem((8 * SIDE, 16 * SIDE), BF16)]
    part, gate, wide, thin, *last = call(
        beside_kernel,
        (
            shape((8 * SIDE, 16 * SIDE), F32),
            shape((BLOCK, CH), F32),
            shape((512, 512), BF16),
            shape((1024, 1024), BF16),
            shape((CH, LANES), F32),
            shape((CH, LANES), F32),
            shape((2 * CH, CH), BF16),
            shape((8, CH), F32),
        ),
        [*operands, *[vmem((1, CH), F32)] * 3, pltpu.SemaphoreType.DMA((5,))],
        in_specs=[here] * 4 + [hbm] * 4,
    )(mine, normed, gate_w, gate_b, *stay((norm_out_gain, norm_out_bias, proj_out, out_bias)))
    triangle = call(
        triangle_kernel,
        shape((2 * CH, SHARE), BF16),
        [*operands, vmem((6, 8 * SIDE, LANES), F32), vmem((SHARE // LANES, 2 * CH, LANES), F32)],
    )(part, got, wide, thin)
    triangle = triangle.reshape(CH, 2, SHARE)
    triangle = lax.all_to_all(
        triangle, ALL, 0, 0, axis_index_groups=groups(), tiled=True
    )
    return call(
        finish_kernel,
        shape((SIDE, SIDE, CH), F32),
        [vmem((SIDE, SIDE, CH), F32), pltpu.SemaphoreType.DMA((32,))],
        out_specs=hbm,
    )(triangle.transpose(1, 0, 2), gate, *last)


def solution(mesh):
    fine = Mesh(mesh.devices.reshape(2, 4, 2, 8, 2), ROW + COL)
    return jax.shard_map(
        body,
        mesh=fine,
        in_specs=(P(ROW, COL, None), P(), P(), P(), P(), P(), P(), P(), P(), P()),
        out_specs=P(ROW, COL, None),
        check_vma=False,
    )
```

```python
import jax
import jax.numpy as jnp
from jax import lax
from jax.experimental import pallas as pl
from jax.experimental.pallas import tpu as pltpu
from jax.sharding import Mesh
from jax.sharding import PartitionSpec as P

CH = 128
ROW = ("y_lo", "x", "core")
COL = ("z", "y_hi")
ALL = ROW + COL
TURN = (4, 7, 1, 2, 6, 0, 5, 3)
PAIRS = (2, 6, 1, 0, 7, 5, 3, 4)
HALVES = (1, 0)
SWAP = [(0, 1), (1, 0)]
LANES = 128
SIDE = 48
PARTS = 1
PART = SIDE // PARTS
WIDE = 32
THIN = 16
BLOCK = SIDE * SIDE
SHARE = BLOCK // 2
PIECE = 3 * LANES
F32 = jnp.float32
BF16 = jnp.bfloat16
EPS = 1e-05


def cat(parts, axis):
    return jnp.concatenate(list(parts), axis=axis)


def across(column):
    return cat([column] * (PIECE // LANES), 1)


def pieces(residues):
    for width, lo in ((WIDE, 0), (THIN, WIDE)):
        count = LANES // width
        n = residues // count
        for v in range(0, n, 3):
            yield [(b * n + u, lo, width) for u in range(v, v + 3) for b in range(count)]


def sides_kernel(
    act_hbm, mask_hbm, gain_hbm, bias_hbm, w_hbm, wb_hbm,
    out_ref, normed_ref, gate_w_ref, gate_b_ref,
    act, mask_v, gain_v, bias_v, w, wb, wt32, wt, wbt, sem,
):
    parts_in = [
        pltpu.make_async_copy(
            act_hbm.at[h * PART : (h + 1) * PART], act.at[h * PART : (h + 1) * PART], sem.at[h]
        )
        for h in range(PARTS)
    ]
    small = [
        pltpu.make_async_copy(src, dst, sem.at[PARTS + n])
        for n, (src, dst) in enumerate(
            (
                (mask_hbm, mask_v.at[0]),
                (gain_hbm, gain_v.at[0]),
                (bias_hbm, bias_v.at[0]),
                (w_hbm, w),
                (wb_hbm, wb.at[0]),
            )
        )
    ]
    for copy in parts_in[:1] + small + parts_in[1:]:
        copy.start()
    total = mask_v.shape[1]
    index = lax.broadcasted_iota(jnp.int32, (total, LANES), 0)
    place = lax.broadcasted_iota(jnp.int32, (total, LANES), 1)
    chosen = [(index == place + lax.axis_index(axis) * SIDE).astype(F32) for axis in (ROW, COL)]
    for copy in small:
        copy.wait()
    known = jnp.broadcast_to(mask_v[...].astype(F32), (8, total))
    row_mask, col_mask = (
        jnp.dot(known, one, preferred_element_type=F32)[:, :SIDE] for one in chosen
    )
    for n in range(4):
        side, kind = divmod(n, 2)
        cols = slice(n * CH, (n + 1) * CH)
        rows = pl.ds(kind * 2 * CH + side, CH, stride=2)
        wt32[rows, :] = w[:, cols].astype(F32).T
        wbt[rows, :] = jnp.broadcast_to(wb[:, cols], (CH, LANES)).T
    wt[...] = wt32[...].astype(BF16)
    gate_w_ref[...] = w[:, 4 * CH :]
    gate_b_ref[...] = jnp.broadcast_to(wb[:, 4 * CH :], gate_b_ref.shape)
    index = lax.broadcasted_iota(jnp.int32, (SIDE, PIECE), 0)
    place = lax.broadcasted_iota(jnp.int32, (SIDE, PIECE), 1)
    for h in range(PARTS):
        parts_in[h].wait()
        for at in range(h * PART, (h + 1) * PART, 8):
            values = act[at : at + 8].reshape(8 * SIDE, LANES)
            off = values - jnp.mean(values, axis=-1, keepdims=True)
            spread = jnp.mean(jnp.square(off), axis=-1, keepdims=True)
            normed = off * lax.rsqrt(spread + EPS) * gain_v[...] + bias_v[...]
            normed_ref[at : at + 8] = normed.astype(BF16).reshape(8, SIDE, LANES)
    for n, piece in enumerate(pieces(SIDE)):
        rows = cat((normed_ref[k, lo : lo + width] for k, lo, width in piece), 0)
        _, lo, width = piece[0]
        step = SIDE * width // LANES
        k_of = piece[0][0] + place // LANES + (place % LANES) // width * step
        mask = jnp.dot(row_mask, (index == k_of).astype(F32), preferred_element_type=F32)
        i_of = lo + place % width
        mask = mask * jnp.dot(col_mask, (index == i_of).astype(F32), preferred_element_type=F32)
        gate, value = (
            lax.dot_general(
                wt[at : at + 2 * CH],
                rows,
                (((1,), (1,)), ((), ())),
                preferred_element_type=F32,
            )
            + across(wbt[at : at + 2 * CH])
            for at in (0, 2 * CH)
        )
        value = mask[:1] * jax.nn.sigmoid(gate) * value
        out_ref[:, n * PIECE : (n + 1) * PIECE] = value.astype(BF16)


def gather_k(values, order, wide, thin, dst_ref):
    blocks = len(order)
    for width, perm, lanes_at, col_at in (
        (WIDE, wide, 0, 0),
        (THIN, thin, SIDE * WIDE, blocks * WIDE),
    ):
        count = LANES // width
        n = SIDE // count
        groups = blocks // count
        left = cat(
            (
                cat(
                    (
                        values[
                            order[m * count + g] * 8 : (order[m * count + g] + 1) * 8,
                            lanes_at + a * LANES : lanes_at + (a + 1) * LANES,
                        ]
                        for g in range(count)
                    ),
                    1,
                )
                for m in range(groups)
                for a in range(n)
            ),
            0,
        ).astype(BF16)
        moved = jnp.dot(left, perm[...], preferred_element_type=F32).astype(BF16)
        for m in range(groups):
            for b in range(count):
                dst_ref[
                    b * n * 8 : (b + 1) * n * 8,
                    col_at + m * LANES : col_at + (m + 1) * LANES,
                ] = moved[m * n * 8 : (m + 1) * n * 8, b * LANES : (b + 1) * LANES]


def product(ref, wide, thin, left_ref, right_ref):
    core, half = lax.axis_index("core"), CH // 2
    start = pl.multiple_of((core if HALVES[0] == 0 else 1 - core) * half, half)
    order = [TURN.index(z) for z in PAIRS]
    gather_k(ref[0, pl.ds(start, half), :].astype(F32), order, wide, thin, left_ref)
    gather_k(ref[1].astype(F32), range(16), wide, thin, right_ref)
    return lax.dot_general(
        left_ref[...], right_ref[...], (((0,), (0,)), ((), ())), preferred_element_type=F32
    )


def build_permutations(wide_ref, thin_ref):
    for ref, width in ((wide_ref, WIDE), (thin_ref, THIN)):
        count = LANES // width
        ref[...] = jnp.zeros(ref.shape, BF16)
        lane = lax.broadcasted_iota(jnp.int32, (width, LANES), 1)
        row = lax.broadcasted_iota(jnp.int32, (width, LANES), 0)
        for g in range(count):
            one = (lane == g * width + row).astype(F32).astype(BF16)
            for b in range(count):
                at = g * LANES + b * width
                ref[at : at + width, b * LANES : (b + 1) * LANES] = one


def beside_kernel(
    mine_ref, normed_ref, w_ref, wb_ref, gain_hbm, bias_hbm, out_w_hbm, out_b_hbm,
    part_ref, gate_ref, wide_ref, thin_ref, gain_ref, bias_ref, twice_ref, out_b_ref,
    left_ref, right_ref, gain_v, bias_v, out_b_v, sem,
):
    copies = [
        pltpu.make_async_copy(src, dst, sem.at[n])
        for n, (src, dst) in enumerate(
            (
                (gain_hbm, gain_v.at[0]),
                (bias_hbm, bias_v.at[0]),
                (out_b_hbm, out_b_v.at[0]),
                (out_w_hbm, twice_ref.at[:CH]),
                (out_w_hbm, twice_ref.at[CH:]),
            )
        )
    ]
    for copy in copies:
        copy.start()
    build_permutations(wide_ref, thin_ref)
    part_ref[...] = product(mine_ref, wide_ref, thin_ref, left_ref, right_ref)
    for n, piece in enumerate(pieces(SIDE)):
        rows = cat((normed_ref[k, lo : lo + width] for k, lo, width in piece), 0)
        lin = jnp.dot(rows, w_ref[...], preferred_element_type=F32) + wb_ref[:1]
        gate_ref[n * PIECE : (n + 1) * PIECE] = jax.nn.sigmoid(lin)
    for copy in copies:
        copy.wait()
    gain_ref[...] = jnp.broadcast_to(gain_v[...], (CH, LANES)).T
    bias_ref[...] = jnp.broadcast_to(bias_v[...], (CH, LANES)).T
    out_b_ref[...] = jnp.broadcast_to(out_b_v[...], out_b_ref.shape)


def triangle_kernel(part_ref, got_ref, wide, thin, out_ref, left_ref, right_ref, tri_ref, out):
    total = part_ref[...] + product(got_ref, wide, thin, left_ref, right_ref)
    for strip in range(6):
        tri_ref[strip] = total[:, strip * LANES : (strip + 1) * LANES]

    def residue(strip, i):
        if i < WIDE:
            return tri_ref[strip, pl.ds(i, 8, stride=WIDE), :]
        return tri_ref[strip, pl.ds(8 * WIDE + i - WIDE, 8, stride=THIN), :]

    for width, perm, lanes_at, strip_at in (
        (WIDE, wide, 0, 0),
        (THIN, thin, SIDE * WIDE, 4),
    ):
        count = LANES // width
        n = SIDE // count
        groups = 16 // count
        left = cat(
            (
                cat((residue(strip_at + m, b * n + a) for b in range(count)), 1)
                for m in range(groups)
                for a in range(n)
            ),
            0,
        ).astype(BF16)
        moved = jnp.dot(left, perm[...], preferred_element_type=F32)
        for m in range(groups):
            for a in range(n):
                rows = moved[(m * n + a) * 8 : (m * n + a + 1) * 8]
                half, lane = divmod(lanes_at + a * LANES, SHARE)
                for g in range(count):
                    to = pl.ds((m * count + g) * 16 + half, 8, stride=2)
                    out[lane // LANES, to, :] = rows[:, g * LANES : (g + 1) * LANES]
    for strip in range(SHARE // LANES):
        out_ref[:, strip * LANES : (strip + 1) * LANES] = out[strip].astype(BF16)


def finish_kernel(tri_ref, gate_ref, gain_ref, bias_ref, twice_ref, wb_ref, out_hbm, out, sem):
    copies = []
    for n, piece in enumerate(pieces(SIDE)):
        half, lane = divmod(n * PIECE, SHARE)
        tri = tri_ref[half, :, lane : lane + PIECE].astype(F32)
        off = tri - jnp.mean(tri, axis=0, keepdims=True)
        spread = jnp.mean(jnp.square(off), axis=0, keepdims=True)
        mixed = off * lax.rsqrt(spread + EPS) * across(gain_ref[...]) + across(bias_ref[...])
        high = mixed.astype(BF16)
        low = (mixed - high.astype(F32)).astype(BF16)
        lin = lax.dot_general(
            cat((high, low), 0),
            twice_ref[...],
            (((0,), (0,)), ((), ())),
            preferred_element_type=F32,
        )
        update = gate_ref[n * PIECE : (n + 1) * PIECE] * (lin + wb_ref[:1])
        for at, (i, lo, width) in enumerate(piece):
            out[i, lo : lo + width] = update[at * width : (at + 1) * width]
        count = len(piece) // 3
        for i, lo, width in piece[:count]:
            where = (slice(i, i + 3), slice(lo, lo + width))
            copy = pltpu.make_async_copy(out.at[where], out_hbm.at[where], sem.at[len(copies)])
            copy.start()
            copies.append(copy)
    for copy in copies:
        copy.wait()


def call(kernel, outs, scratch=(), cost=10**9, **options):
    return pl.pallas_call(
        kernel,
        out_shape=outs,
        scratch_shapes=scratch,
        compiler_params=pltpu.CompilerParams(vmem_limit_bytes=40 * 2**20),
        cost_estimate=pl.CostEstimate(flops=cost, bytes_accessed=3 * 10**6, transcendentals=0),
        **options,
    )


def groups():
    chips = [
        [(pair * 2 + core) * 16 + z * 2 + y_hi for core in range(2)]
        for y_hi in HALVES
        for z in TURN
        for pair in PAIRS
    ]
    return [[chip[core] for chip in chips] for core in range(2)]


def stay(arrays):
    return [pltpu.with_memory_space_constraint(x, pltpu.HBM) for x in arrays]


def body(
    pair_act,
    residue_mask,
    norm_in_gain,
    norm_in_bias,
    proj_in,
    proj_bias,
    norm_out_gain,
    norm_out_bias,
    proj_out,
    out_bias,
):
    shape = jax.ShapeDtypeStruct
    vmem = pltpu.VMEM
    total = residue_mask.shape[0]
    hbm, here = pl.BlockSpec(memory_space=pltpu.HBM), pl.BlockSpec(memory_space=vmem)
    sides, normed, gate_w, gate_b = call(
        sides_kernel,
        (
            shape((2 * CH, BLOCK), BF16),
            shape((SIDE, SIDE, CH), BF16),
            shape((CH, CH), BF16),
            shape((8, CH), F32),
        ),
        [
            vmem((SIDE, SIDE, CH), F32),
            vmem((1, total), jnp.int32),
            vmem((1, CH), F32),
            vmem((1, CH), F32),
            vmem((CH, 5 * CH), BF16),
            vmem((1, 5 * CH), F32),
            vmem((4 * CH, CH), F32),
            vmem((4 * CH, CH), BF16),
            vmem((4 * CH, LANES), F32),
            pltpu.SemaphoreType.DMA((PARTS + 5,)),
        ],
        in_specs=[hbm] * 6,
    )(*stay((pair_act, residue_mask, norm_in_gain, norm_in_bias, proj_in, proj_bias)))
    packed = sides.reshape(CH, 2, BLOCK)
    packed = lax.all_to_all(packed, ALL, 0, 0, axis_index_groups=groups(), tiled=True)
    mine = packed.transpose(1, 0, 2)
    got = lax.ppermute(mine, "core", SWAP)
    operands = [vmem((8 * SIDE, 8 * SIDE), BF16), vmem((8 * SIDE, 16 * SIDE), BF16)]
    part, gate, wide, thin, *last = call(
        beside_kernel,
        (
            shape((8 * SIDE, 16 * SIDE), F32),
            shape((BLOCK, CH), F32),
            shape((512, 512), BF16),
            shape((1024, 1024), BF16),
            shape((CH, LANES), F32),
            shape((CH, LANES), F32),
            shape((2 * CH, CH), BF16),
            shape((8, CH), F32),
        ),
        [*operands, *[vmem((1, CH), F32)] * 3, pltpu.SemaphoreType.DMA((5,))],
        in_specs=[here] * 4 + [hbm] * 4,
    )(mine, normed, gate_w, gate_b, *stay((norm_out_gain, norm_out_bias, proj_out, out_bias)))
    triangle = call(
        triangle_kernel,
        shape((2 * CH, SHARE), BF16),
        [*operands, vmem((6, 8 * SIDE, LANES), F32), vmem((SHARE // LANES, 2 * CH, LANES), F32)],
    )(part, got, wide, thin)
    triangle = triangle.reshape(CH, 2, SHARE)
    triangle = lax.all_to_all(
        triangle, ALL, 0, 0, axis_index_groups=groups(), tiled=True
    )
    return call(
        finish_kernel,
        shape((SIDE, SIDE, CH), F32),
        [vmem((SIDE, SIDE, CH), F32), pltpu.SemaphoreType.DMA((32,))],
        out_specs=hbm,
    )(triangle.transpose(1, 0, 2), gate, *last)


def solution(mesh):
    fine = Mesh(mesh.devices.reshape(2, 4, 2, 8, 2), ROW + COL)
    return jax.shard_map(
        body,
        mesh=fine,
        in_specs=(P(ROW, COL, None), P(), P(), P(), P(), P(), P(), P(), P(), P()),
        out_specs=P(ROW, COL, None),
        check_vma=False,
    )
```
